128 devices in a mesh: dp: 16 (over y, z_lo, core), section: 8 (over x, z_hi).
Axes of the slice: x: 4, y: 4, z: 4 (z_hi: 2, z_lo: 2; z = z_hi * 2 + z_lo), core: 2. Of those that a mesh axis runs over, the one named last changes fastest.
Arguments:
- enc_states: bfloat16 [4096, 4096], P('dp', 'section'), may hold values from -6 to 6
- queries: bfloat16 [8, 6144, 2048], P('section', 'dp'), may hold values from -40 to 40
- cotangent: bfloat16 [8, 6144, 2048], P('section', 'dp'), may hold values from -24 to 24
- enc_lengths: int32 [16], P('dp'), may hold values from 64 to 256, as said below
- key_weight: bfloat16 [8, 4096, 2048], P('section', 'dp'), may hold values from -0.09375 to 0.09375
- value_weight: bfloat16 [8, 4096, 2048], P('section', 'dp'), may hold values from -0.09375 to 0.09375
- key_down: bfloat16 [8, 4096, 16], P('section'), may hold values from -0.09375 to 0.09375
- key_up: bfloat16 [8, 16, 2048], P('section'), may hold values from -1.5 to 1.5
- value_down: bfloat16 [8, 4096, 16], P('section'), may hold values from -0.09375 to 0.09375
- value_up: bfloat16 [8, 16, 2048], P('section'), may hold values from -1.5 to 1.5
Outputs:
- enc_grad: bfloat16 [4096, 4096], P('dp', 'section')
- key_down_grad: float32 [8, 4096, 16], P('section')
- key_up_grad: float32 [8, 16, 2048], P('section')
- value_down_grad: float32 [8, 4096, 16], P('section')
- value_up_grad: float32 [8, 16, 2048], P('section')
The draws below stay inside these ranges and needn't reach their ends.
Inputs may be any that keep to these rules, and one draw needn't show every extreme that they name: `enc_lengths`: some sequence has 256 and some 256 // 4 unpadded tokens.
All inputs are finite; a program needn't handle non-finite values.
Results may differ from the reference program's by a relative error of at most 0.03.
The reference program's roundings to bfloat16 on the way count: a program that leaves them out, or rounds other values in their place, can miss the bound.
Values may be sent and summed in bfloat16 or wider, within the bound.
A program may use at most 192 MiB of HBM per device.

```python
import jax
import jax.numpy as jnp
from jax import lax

D = 4096
HEADS = 32
HEAD_DIM = 64
RANK = 16
ENC_LEN = 256
DEC_LEN = 384
INNER = 2048
ENC_ROWS = 4096
DEC_ROWS = 6144
N_DP = 16
N_SECTION = 8


def draw_queries(key, part):
    key = jax.random.fold_in(key, 11)
    base = jnp.clip(jax.random.normal(key, (N_SECTION, DEC_LEN * N_DP, HEADS * HEAD_DIM), jnp.float32), -4.0, 4.0) * 0.15
    return base.astype(jnp.bfloat16)


def draw_enc_lengths(key, part):
    key = jax.random.fold_in(key, 5)
    drawn = jax.random.randint(key, (N_DP,), ENC_LEN // 4, ENC_LEN + 1)
    drawn = drawn.at[0].set(ENC_LEN)
    return drawn.at[1].set(ENC_LEN // 4).astype(jnp.int32)


def level_of(key, shape, pieces, smallest, top_value):
    def one(axis_at, parts):
        draws = jax.random.uniform(jax.random.fold_in(jax.random.fold_in(key, 6), axis_at), (parts,), jnp.float32, smallest / len(pieces), top_value / len(pieces))
        return jnp.repeat(jnp.exp(draws), shape[axis_at] // parts).reshape((-1,) + (1,) * (len(shape) - axis_at - 1))

    level = one(*pieces[0])
    for cut in pieces[1:]:
        level = level * one(*cut)
    return level


def scatter_about(own_key, dims, scale, limit, shards=(), dtype=jnp.bfloat16):
    entries = scale * jax.random.normal(own_key, dims, jnp.float32)
    if shards:
        entries = entries * level_of(own_key, dims, shards, -0.22, 0.18)
    return jnp.clip(entries, -limit, limit).astype(dtype)


def setup_inputs(seed: int = 0) -> dict:
    keys = jax.random.split(jax.random.key(seed), 11)
    enc_states = scatter_about(keys[0], (ENC_ROWS, D), 1.0, 6.0, ((0, 16), (1, 8)))
    queries = draw_queries(jax.random.fold_in(keys[10], 71), 0)
    cotangent = scatter_about(keys[2], (N_SECTION, DEC_ROWS, INNER), 4.0, 24.0, ((0, 8), (1, 16)))
    enc_lengths = draw_enc_lengths(jax.random.fold_in(keys[10], 71), 0)
    key_weight = scatter_about(keys[4], (N_SECTION, D, INNER), D ** -0.5, 0.09375, ((0, 8), (1, 16)))
    value_weight = scatter_about(keys[5], (N_SECTION, D, INNER), D ** -0.5, 0.09375, ((0, 8), (1, 16)))
    key_down = scatter_about(keys[6], (N_SECTION, D, RANK), D ** -0.5, 0.09375, ((0, 8),))
    key_up = scatter_about(keys[7], (N_SECTION, RANK, INNER), RANK ** -0.5, 1.5, ((0, 8),))
    value_down = scatter_about(keys[8], (N_SECTION, D, RANK), D ** -0.5, 0.09375, ((0, 8),))
    value_up = scatter_about(keys[9], (N_SECTION, RANK, INNER), RANK ** -0.5, 1.5, ((0, 8),))
    return {"enc_states": enc_states, "queries": queries, "cotangent": cotangent, "enc_lengths": enc_lengths, "key_weight": key_weight, "value_weight": value_weight, "key_down": key_down, "key_up": key_up, "value_down": value_down, "value_up": value_up}


adapter_scale = 0.5
masked_score = -1e30


def project(encoded, weight, down, up):
    base = jnp.dot(encoded, weight, preferred_element_type=jnp.float32)
    low_rank = jnp.dot(encoded, down, preferred_element_type=jnp.float32).astype(jnp.bfloat16)
    summed = base + adapter_scale * jnp.dot(low_rank, up, preferred_element_type=jnp.float32)
    return summed.astype(jnp.bfloat16), low_rank


def adapter_back(encoded, gradient, low_rank, weight, down, up):
    up_grad = adapter_scale * jnp.dot(low_rank.T, gradient, preferred_element_type=jnp.float32)
    low_grad = (adapter_scale * jnp.dot(gradient, up.T, preferred_element_type=jnp.float32)).astype(jnp.bfloat16)
    down_grad = jnp.dot(encoded.T, low_grad, preferred_element_type=jnp.float32)
    through = jnp.dot(gradient, weight.T, preferred_element_type=jnp.float32)
    through = through + jnp.dot(low_grad, down.T, preferred_element_type=jnp.float32)
    return through, down_grad, up_grad


def layer_backward(encoded, query_rows, grad_rows, length, key_weight, value_weight, key_down, key_up, value_down, value_up):
    head_count = query_rows.shape[1] // HEAD_DIM
    key_rows, key_low = project(encoded, key_weight, key_down, key_up)
    value_rows, value_low = project(encoded, value_weight, value_down, value_up)
    query_heads = query_rows.reshape(-1, head_count, HEAD_DIM).astype(jnp.float32)
    key_heads = key_rows.reshape(-1, head_count, HEAD_DIM).astype(jnp.float32)
    value_heads = value_rows.reshape(-1, head_count, HEAD_DIM).astype(jnp.float32)
    grad_heads = grad_rows.reshape(-1, head_count, HEAD_DIM).astype(jnp.float32)
    scores = jnp.einsum("qhd,khd->hqk", query_heads, key_heads)
    visible = jnp.arange(encoded.shape[0]) < length
    scores = jnp.where(visible[None, None, :], scores, masked_score)
    peak_score = jnp.max(scores, axis=2, keepdims=True)
    expo = jnp.exp(scores - peak_score)
    probs = (expo / jnp.sum(expo, axis=2, keepdims=True)).astype(jnp.bfloat16).astype(jnp.float32)
    attended = jnp.einsum("hqk,khd->qhd", probs, value_heads)
    row_inner = jnp.sum(attended * grad_heads, axis=2)
    dprobs = jnp.einsum("qhd,khd->hqk", grad_heads, value_heads)
    dscores = (probs * (dprobs - row_inner.T[:, :, None])).astype(jnp.bfloat16).astype(jnp.float32)
    dvalues = jnp.einsum("hqk,qhd->khd", probs, grad_heads).reshape(encoded.shape[0], -1).astype(jnp.bfloat16)
    dkeys = jnp.einsum("hqk,qhd->khd", dscores, query_heads).reshape(encoded.shape[0], -1).astype(jnp.bfloat16)
    key_through, key_down_grad, key_up_grad = adapter_back(encoded, dkeys, key_low, key_weight, key_down, key_up)
    value_through, value_down_grad, value_up_grad = adapter_back(encoded, dvalues, value_low, value_weight, value_down, value_up)
    partial_value = (key_through + value_through).astype(jnp.bfloat16)
    return partial_value, key_down_grad, key_up_grad, value_down_grad, value_up_grad


def reference(enc_states, queries, cotangent, enc_lengths, key_weight, value_weight, key_down, key_up, value_down, value_up):
    encoded = enc_states.reshape(N_DP, ENC_LEN, D)
    summed = jnp.zeros((N_DP, ENC_LEN, D), jnp.float32)
    outs = ([], [], [], [])
    for layer_index in range(N_SECTION):
        query_seq = queries[layer_index].reshape(N_DP, DEC_LEN, -1)
        grad_seq = cotangent[layer_index].reshape(N_DP, DEC_LEN, -1)

        def per_sequence(inputs):
            return layer_backward(inputs[0], inputs[1], inputs[2], inputs[3], key_weight[layer_index], value_weight[layer_index], key_down[layer_index], key_up[layer_index], value_down[layer_index], value_up[layer_index])

        partial_value, kdg, kug, vdg, vug = lax.map(per_sequence, (encoded, query_seq, grad_seq, enc_lengths))
        summed = summed + partial_value.astype(jnp.float32)
        outs[0].append(jnp.sum(kdg, axis=0))
        outs[1].append(jnp.sum(kug, axis=0))
        outs[2].append(jnp.sum(vdg, axis=0))
        outs[3].append(jnp.sum(vug, axis=0))
    enc_grad = summed.reshape(N_DP * ENC_LEN, D).astype(jnp.bfloat16)
    return (enc_grad, jnp.stack(outs[0]), jnp.stack(outs[1]), jnp.stack(outs[2]), jnp.stack(outs[3]))
```

```python
import functools

import jax
import jax.numpy as jnp
from jax import lax
from jax.experimental import pallas as pl
from jax.experimental.pallas import tpu as pltpu
from jax.sharding import PartitionSpec as P

HEAD_DIM = 64
MESH = pl.DeviceIdType.MESH
adapter_scale = 0.5
masked_score = -1e30
F32 = jnp.float32
BF16 = jnp.bfloat16

CHUNK = 256
BLOCK = 256
V_ZFIRST = 1

NT = (((1,), (1,)), ((), ()))
TN = (((0,), (0,)), ((), ()))


def dot_nt(a, b):
    return lax.dot_general(a, b, NT, preferred_element_type=F32)


def dot_tn(a, b):
    return lax.dot_general(a, b, TN, preferred_element_type=F32)


def kernel(
    chunks,
    enc_hbm, q_hbm, g_hbm, len_ref, kw_hbm, vw_hbm, kd_hbm, ku_hbm, vd_hbm, vu_hbm,
    out_ref, adapt_ref,
    W, E, Q, G, down, up, low, lowg, dkv, stage, out_recv, A, A_recv, A_all,
    local_sem, own_sem, w_send, w_recv, e_send, e_recv, o_send, o_recv, r_send, r_recv, a_send, a_recv,
):
    dp = lax.axis_index("dp")
    sec = lax.axis_index("section")
    c, zl, y = lax.rem(dp, 2), lax.rem(dp // 2, 2), dp // 4
    yp, ym, yo = lax.rem(y + 1, 4), lax.rem(y + 3, 4), lax.rem(y + 2, 4)

    def did(y_, z_, c_):
        return ((y_ * 2 + z_) * 2 + c_, sec)

    UP, DN, ZM, CM = did(yp, zl, c), did(ym, zl, c), did(y, 1 - zl, c), did(y, zl, 1 - c)

    def dp_peer(o):
        return lax.rem(dp + o, 16)

    def sec_peer(o):
        return lax.rem(sec + o, 8)

    barrier = pltpu.get_barrier_semaphore()
    for o in range(1, 16):
        pl.semaphore_signal(barrier, inc=1, device_id=(dp_peer(o), sec), device_id_type=MESH)
    for o in range(1, 8):
        pl.semaphore_signal(barrier, inc=1, device_id=(dp, sec_peer(o)), device_id_type=MESH)

    own = []
    for t, w in enumerate((kw_hbm, vw_hbm)):
        for j in range(chunks):
            own.append(
                pltpu.make_async_copy(
                    w.at[0, :, pl.ds(j * CHUNK, CHUNK)], W.at[t, j, y, zl, c], own_sem.at[t, j]
                )
            )
    columns = enc_hbm.shape[1]
    own_columns = pl.ds(pl.multiple_of(sec * columns, columns), columns)
    local = [
        pltpu.make_async_copy(enc_hbm, E.at[:, own_columns], local_sem.at[0]),
        pltpu.make_async_copy(q_hbm.at[0], Q, local_sem.at[1]),
        pltpu.make_async_copy(g_hbm.at[0], G, local_sem.at[2]),
        pltpu.make_async_copy(kd_hbm.at[0], down.at[0], local_sem.at[3]),
        pltpu.make_async_copy(vd_hbm.at[0], down.at[1], local_sem.at[4]),
        pltpu.make_async_copy(ku_hbm.at[0], up.at[0], local_sem.at[5]),
        pltpu.make_async_copy(vu_hbm.at[0], up.at[1], local_sem.at[6]),
    ]
    for copy in own + local:
        copy.start()
    for copy in own:
        copy.wait()
    pl.semaphore_wait(barrier, 22)

    def enc_copy(o):
        return pltpu.make_async_remote_copy(
            src_ref=enc_hbm, dst_ref=E.at[:, own_columns], send_sem=e_send.at[o], recv_sem=e_recv.at[o],
            device_id=(dp, sec_peer(o)), device_id_type=MESH,
        )

    def enc_arrival(o):
        src = lax.rem(sec + 8 - o, 8)
        cols = pl.ds(pl.multiple_of(src * columns, columns), columns)
        return pltpu.make_async_remote_copy(
            src_ref=enc_hbm, dst_ref=E.at[:, cols], send_sem=e_send.at[o], recv_sem=e_recv.at[o],
            device_id=(dp, src), device_id_type=MESH,
        )

    for o in range(1, 8):
        enc_copy(o).start()

    def rcopy(t, j, n, dev, ref):
        return pltpu.make_async_remote_copy(
            src_ref=ref, dst_ref=ref, send_sem=w_send.at[t, j, n], recv_sem=w_recv.at[t, j, n],
            device_id=dev, device_id_type=MESH,
        )

    def blk(t, j, y_, z_):
        return W.at[t, j, y_, z_, c]

    def pair(t, j, y_, c_):
        return W.at[t, j, y_, :, c_]

    def half(t, j, y_, h):
        return W.at[t, j, y_, zl, c, pl.ds(128 * h, 128)]

    def out(t, j, n, zf):
        if n == 0:
            return rcopy(t, j, n, ZM, blk(t, j, y, zl))
        if n in (1, 2):
            return rcopy(t, j, n, UP if n == 1 else DN, pair(t, j, y, c) if zf else blk(t, j, y, zl))
        if n == 3:
            return rcopy(t, j, n, UP, blk(t, j, ym, 0) if zf else half(t, j, ym, 0))
        if n == 4:
            return rcopy(t, j, n, DN, blk(t, j, yp, 1) if zf else half(t, j, yp, 1))
        if n <= 8:
            return rcopy(t, j, n, CM, pair(t, j, (y, ym, yp, yo)[n - 5], c))
        return rcopy(t, j, n, ZM, blk(t, j, (ym, yp, yo)[n - 9], zl))

    def inc(t, j, n, zf):
        if n == 0:
            return rcopy(t, j, n, ZM, blk(t, j, y, 1 - zl))
        if n in (1, 2):
            y_ = ym if n == 1 else yp
            return rcopy(t, j, n, DN if n == 1 else UP, pair(t, j, y_, c) if zf else blk(t, j, y_, zl))
        if n == 3:
            return rcopy(t, j, n, DN, blk(t, j, yo, 0) if zf else half(t, j, yo, 0))
        if n == 4:
            return rcopy(t, j, n, UP, blk(t, j, yo, 1) if zf else half(t, j, yo, 1))
        if n <= 8:
            return rcopy(t, j, n, CM, pair(t, j, (y, ym, yp, yo)[n - 5], 1 - c))
        return rcopy(t, j, n, ZM, blk(t, j, (ym, yp, yo)[n - 9], 1 - zl))

    def go(t, j, zf, *ns):
        for n in ns:
            out(t, j, n, zf).start()

    def wt(t, j, zf, *ns):
        for n in ns:
            inc(t, j, n, zf).wait_recv()

    def st1(t, j, zf):
        if zf:
            go(t, j, zf, 0)
        else:
            go(t, j, zf, 1, 2, 0)

    def st2(t, j, zf):
        if zf:
            wt(t, j, zf, 0)
            go(t, j, zf, 1, 2, 5)
        else:
            wt(t, j, zf, 1, 2)
            go(t, j, zf, 3, 4, 9, 10)
            wt(t, j, zf, 0)
            go(t, j, zf, 5)

    def st3(t, j, zf):
        if zf:
            wt(t, j, zf, 1, 2)
            go(t, j, zf, 3, 4, 6, 7)
        else:
            wt(t, j, zf, 3, 4)
            go(t, j, zf, 11)
            wt(t, j, zf, 9, 10)
            go(t, j, zf, 6, 7)

    def st4(t, j, zf):
        wt(t, j, zf, *((3, 4) if zf else (11,)))
        go(t, j, zf, 8)

    def st5(t, j, zf):
        wt(t, j, zf, 5, 6, 7, 8)

    def sent(t, j, zf):
        for n in range(9 if zf else 12):
            out(t, j, n, zf).wait_send()

    def routed(fn, j):
        fn(0, j, True)

        @pl.when(j >= chunks - V_ZFIRST)
        def _():
            fn(1, j, True)

        @pl.when(j < chunks - V_ZFIRST)
        def _():
            fn(1, j, False)

    def first():
        for copy in local:
            copy.wait()
        for o in range(1, 8):
            enc_arrival(o).wait_recv()
        for t in range(2):
            low[t] = jnp.dot(E[...], down[t], preferred_element_type=F32).astype(BF16)
            lowg[t] = jnp.zeros(lowg.shape[1:], F32)

    def compute(j):
        cols = pl.ds(pl.multiple_of(j * CHUNK, CHUNK), CHUNK)
        rows = []
        for t in range(2):
            weight = W[t, j].reshape(16 * BLOCK, CHUNK)
            base = jnp.dot(E[...], weight, preferred_element_type=F32)
            base = base + adapter_scale * jnp.dot(low[t], up[t, :, cols], preferred_element_type=F32)
            rows.append(base.astype(BF16))
        key_rows, value_rows = rows
        q, g = Q[:, cols], G[:, cols]
        lane = lax.broadcasted_iota(jnp.int32, (1, CHUNK), 1) // HEAD_DIM
        visible = lax.broadcasted_iota(jnp.int32, (BLOCK, 1), 0) < len_ref[0]
        dkeys = jnp.zeros((BLOCK, CHUNK), F32)
        dvalues = jnp.zeros((BLOCK, CHUNK), F32)
        zero = jnp.zeros((), BF16)
        for h in range(CHUNK // HEAD_DIM):
            here = lane == h
            scores = dot_nt(jnp.where(here, key_rows, zero), q)
            scores = jnp.where(visible, scores, masked_score)
            expo = jnp.exp(scores - jnp.max(scores, axis=0, keepdims=True))
            probs = (expo * (1.0 / jnp.sum(expo, axis=0, keepdims=True))).astype(BF16)
            dprobs = dot_nt(jnp.where(here, value_rows, zero), g)
            wide = probs.astype(F32)
            inner = jnp.sum(wide * dprobs, axis=0, keepdims=True)
            dscores = (wide * (dprobs - inner)).astype(BF16)
            dvalues = jnp.where(here, jnp.dot(probs, g, preferred_element_type=F32), dvalues)
            dkeys = jnp.where(here, jnp.dot(dscores, q, preferred_element_type=F32), dkeys)
        for t, grad in enumerate((dkeys, dvalues)):
            grad = grad.astype(BF16)
            dkv[t, j] = grad
            lowg[t] += dot_nt(grad, up[t, :, cols])
            up_grad = adapter_scale * dot_tn(low[t], grad)
            for half_ in range(2):
                A[2 * j + half_, pl.ds(16 * t, 16), 256:384] = up_grad[:, 128 * half_ : 128 * half_ + 128]

    def slot(k, carry):
        for i, fn in enumerate((st1, st2, st3, st4, st5)):
            j = k - i

            @pl.when(jnp.logical_and(j >= 0, j < chunks))
            def _(fn=fn, j=j):
                routed(fn, j)

        @pl.when(k == 4)
        def _():
            first()

        @pl.when(k >= 4)
        def _():
            compute(k - 4)

        return carry

    lax.fori_loop(0, chunks + 4, slot, 0)

    for t in range(2):
        low[t] = (adapter_scale * lowg[t]).astype(BF16)

    def down_grad(r, carry):
        e = E[:, pl.ds(pl.multiple_of(r * BLOCK, BLOCK), BLOCK)]
        for t in range(2):
            A[r, pl.ds(16 * t, 16), 0:256] = dot_tn(low[t], e)
        return carry

    lax.fori_loop(0, 16, down_grad, 0)

    def reduce_copy(o):
        return pltpu.make_async_remote_copy(
            src_ref=A.at[dp_peer(o)], dst_ref=A_recv.at[o], send_sem=r_send.at[o], recv_sem=r_recv.at[o],
            device_id=(dp_peer(o), sec), device_id_type=MESH,
        )

    for o in range(1, 16):
        reduce_copy(o).start()

    def partial_copy(o):
        return pltpu.make_async_remote_copy(
            src_ref=stage.at[o], dst_ref=out_recv.at[o], send_sem=o_send.at[o], recv_sem=o_recv.at[o],
            device_id=(dp, sec_peer(o)), device_id_type=MESH,
        )

    def back(i, carry):
        o = i + 1
        p = lax.rem(sec + o, 8)
        for b in range(2):
            r = 2 * p + b
            r_y, r_z, r_c = r // 4, lax.rem(r // 2, 2), lax.rem(r, 2)
            acc = jnp.zeros((BLOCK, BLOCK), F32)
            for t in range(2):
                wide = jnp.concatenate([W[t, j, r_y, r_z, r_c] for j in range(chunks)], axis=1)
                grad = jnp.concatenate([dkv[t, j] for j in range(chunks)], axis=1)
                acc = acc + dot_nt(grad, wide)
                d = down[t, pl.ds(pl.multiple_of(r * BLOCK, BLOCK), BLOCK), :]
                acc = acc + dot_nt(low[t], d)
            stage[lax.rem(o, 8), :, b * BLOCK : (b + 1) * BLOCK] = acc.astype(BF16)

        @pl.when(o < 8)
        def _():
            partial_copy(o).start()

        return carry

    lax.fori_loop(0, 8, back, 0)

    total = A[dp]
    for o in range(1, 16):
        reduce_copy(o).wait_recv()
        total = total + A_recv[o]
    A_all[dp] = total

    def spread_copy(o, index):
        return pltpu.make_async_remote_copy(
            src_ref=A_all.at[index], dst_ref=A_all.at[index], send_sem=a_send.at[o], recv_sem=a_recv.at[o],
            device_id=(dp_peer(o), sec), device_id_type=MESH,
        )

    for o in range(1, 16):
        spread_copy(o, dp).start()

    summed = stage[0].astype(F32)
    for o in range(1, 8):
        partial_copy(o).wait_recv()
        summed = summed + out_recv[o].astype(F32)
    out_ref[...] = summed.astype(BF16)

    for o in range(1, 16):
        spread_copy(o, lax.rem(dp + 16 - o, 16)).wait_recv()
    adapt_ref[...] = A_all[...]

    def drain(j, carry):
        routed(sent, j)
        return carry

    lax.fori_loop(0, chunks, drain, 0)
    for o in range(1, 8):
        enc_copy(o).wait_send()
        partial_copy(o).wait_send()
    for o in range(1, 16):
        reduce_copy(o).wait_send()
        spread_copy(o, dp).wait_send()


def per_device(
    enc_states, queries, cotangent, enc_lengths, key_weight, value_weight, key_down, key_up, value_down, value_up
):
    inner = queries.shape[2]
    chunks = inner // CHUNK
    width = key_down.shape[1]
    columns = enc_states.shape[1]
    hbm = pl.BlockSpec(memory_space=pl.ANY)
    vmem = pl.BlockSpec(memory_space=pltpu.VMEM)
    dma = pltpu.SemaphoreType.DMA
    out, adapt = pl.pallas_call(
        functools.partial(kernel, chunks),
        out_shape=(
            jax.ShapeDtypeStruct((BLOCK, columns), BF16),
            jax.ShapeDtypeStruct((16, 32, 384), F32),
        ),
        in_specs=[hbm, hbm, hbm, pl.BlockSpec(memory_space=pltpu.SMEM)] + [hbm] * 6,
        out_specs=(vmem, vmem),
        scratch_shapes=[
            pltpu.VMEM((2, chunks, 4, 2, 2, BLOCK, CHUNK), BF16),
            pltpu.VMEM((BLOCK, width), BF16),
            pltpu.VMEM(queries.shape[1:], BF16),
            pltpu.VMEM(cotangent.shape[1:], BF16),
            pltpu.VMEM((2, width, 16), BF16),
            pltpu.VMEM((2, 16, inner), BF16),
            pltpu.VMEM((2, BLOCK, 16), BF16),
            pltpu.VMEM((2, BLOCK, 16), F32),
            pltpu.VMEM((2, chunks, BLOCK, CHUNK), BF16),
            pltpu.VMEM((8, BLOCK, columns), BF16),
            pltpu.VMEM((8, BLOCK, columns), BF16),
            pltpu.VMEM((16, 32, 384), F32),
            pltpu.VMEM((16, 32, 384), F32),
            pltpu.VMEM((16, 32, 384), F32),
            dma((7,)),
            dma((2, chunks)),
            dma((2, chunks, 12)),
            dma((2, chunks, 12)),
            dma((8,)),
            dma((8,)),
            dma((8,)),
            dma((8,)),
            dma((16,)),
            dma((16,)),
            dma((16,)),
            dma((16,)),
        ],
        compiler_params=pltpu.CompilerParams(
            collective_id=0, has_side_effects=True, vmem_limit_bytes=60 * 1024 * 1024
        ),
        name="adapter_backward",
    )(
        enc_states, queries, cotangent, enc_lengths, key_weight, value_weight, key_down, key_up, value_down, value_up
    )
    down_grads = jnp.transpose(adapt[:, :, :256].reshape(16, 2, 16, 256), (1, 0, 3, 2)).reshape(2, 1, width, 16)
    up_grads = jnp.transpose(adapt[:, :, 256:].reshape(16, 2, 16, 128), (1, 2, 0, 3)).reshape(2, 1, 16, inner)
    return out, down_grads[0], up_grads[0], down_grads[1], up_grads[1]


def solution(mesh):
    return jax.shard_map(
        per_device,
        mesh=mesh,
        in_specs=(
            P("dp", "section"),
            P("section", "dp", None),
            P("section", "dp", None),
            P("dp"),
            P("section", "dp", None),
            P("section", "dp", None),
            P("section", None, None),
            P("section", None, None),
            P("section", None, None),
            P("section", None, None),
        ),
        out_specs=(
            P("dp", "section"),
            P("section", None, None),
            P("section", None, None),
            P("section", None, None),
            P("section", None, None),
        ),
        check_vma=False,
    )
```

```python
import functools

import jax
import jax.numpy as jnp
from jax import lax
from jax.experimental import pallas as pl
from jax.experimental.pallas import tpu as pltpu
from jax.sharding import PartitionSpec as P

HEAD_DIM = 64
MESH = pl.DeviceIdType.MESH
adapter_scale = 0.5
masked_score = -1e30
F32 = jnp.float32
BF16 = jnp.bfloat16

CHUNK = 256
BLOCK = 256
V_ZFIRST = 1

NT = (((1,), (1,)), ((), ()))
TN = (((0,), (0,)), ((), ()))


def dot_nt(a, b):
    return lax.dot_general(a, b, NT, preferred_element_type=F32)


def dot_tn(a, b):
    return lax.dot_general(a, b, TN, preferred_element_type=F32)


def kernel(
    chunks,
    enc_hbm, q_hbm, g_hbm, len_ref, kw_hbm, vw_hbm, kd_hbm, ku_hbm, vd_hbm, vu_hbm,
    out_ref, kd_ref, ku_ref, vd_ref, vu_ref,
    W, E, Q, G, down, up, low, lowg, dkv, stage, out_recv, cross, cross_recv, A, A_recv, A_all,
    local_sem, own_sem, w_send, w_recv, e_send, e_recv, o_send, o_recv, r_send, r_recv, a_send, a_recv,
):
    dp = lax.axis_index("dp")
    sec = lax.axis_index("section")
    c, zl, y = lax.rem(dp, 2), lax.rem(dp // 2, 2), dp // 4
    yp, ym, yo = lax.rem(y + 1, 4), lax.rem(y + 3, 4), lax.rem(y + 2, 4)

    def did(y_, z_, c_):
        return ((y_ * 2 + z_) * 2 + c_, sec)

    UP, DN, ZM, CM = did(yp, zl, c), did(ym, zl, c), did(y, 1 - zl, c), did(y, zl, 1 - c)

    def dp_peer(o):
        return lax.rem(dp + o, 16)

    x, zh = sec // 2, lax.rem(sec, 2)

    def sec_at(dx, other):
        return lax.rem(x + dx, 4) * 2 + (1 - zh if other else zh)

    barrier = pltpu.get_barrier_semaphore()
    for o in range(1, 16):
        pl.semaphore_signal(barrier, inc=1, device_id=(dp_peer(o), sec), device_id_type=MESH)
    for to in (sec_at(0, True), sec_at(1, False), sec_at(2, False), sec_at(3, False)):
        pl.semaphore_signal(barrier, inc=1, device_id=(dp, to), device_id_type=MESH)

    own = []
    for t, w in enumerate((kw_hbm, vw_hbm)):
        for j in range(chunks):
            own.append(
                pltpu.make_async_copy(
                    w.at[0, :, pl.ds(j * CHUNK, CHUNK)], W.at[t, j, y, zl, c], own_sem.at[t, j]
                )
            )
    columns = enc_hbm.shape[1]

    def section_columns(p):
        return pl.ds(pl.multiple_of(p * columns, columns), columns)

    local = [
        pltpu.make_async_copy(enc_hbm, E.at[:, section_columns(sec)], local_sem.at[0]),
        pltpu.make_async_copy(q_hbm.at[0], Q, local_sem.at[1]),
        pltpu.make_async_copy(g_hbm.at[0], G, local_sem.at[2]),
        pltpu.make_async_copy(kd_hbm, down.at[0], local_sem.at[3]),
        pltpu.make_async_copy(vd_hbm, down.at[1], local_sem.at[4]),
        pltpu.make_async_copy(ku_hbm.at[0], up.at[0], local_sem.at[5]),
        pltpu.make_async_copy(vu_hbm.at[0], up.at[1], local_sem.at[6]),
    ]
    for copy in own + local:
        copy.start()
    pl.semaphore_wait(barrier, 19)

    def enc_copy(n, src_ref, piece, to):
        return pltpu.make_async_remote_copy(
            src_ref=src_ref, dst_ref=E.at[:, section_columns(piece)], send_sem=e_send.at[n], recv_sem=e_recv.at[n],
            device_id=(dp, to), device_id_type=MESH,
        )

    def enc_out(n):
        if n == 0:
            return enc_copy(n, enc_hbm, sec, sec_at(0, True))
        if n < 4:
            return enc_copy(n, enc_hbm, sec, sec_at(n, False))
        mate = sec_at(0, True)
        return enc_copy(n, E.at[:, section_columns(mate)], mate, sec_at(n - 3, False))

    def enc_in(n):
        if n == 0:
            piece = sec_at(0, True)
        else:
            piece = sec_at(4 - n, False) if n < 4 else sec_at(7 - n, True)
        return enc_copy(n, E.at[:, section_columns(piece)], piece, sec_at(0, True))

    for n in range(4):
        enc_out(n).start()

    def rcopy(t, j, n, dev, ref):
        return pltpu.make_async_remote_copy(
            src_ref=ref, dst_ref=ref, send_sem=w_send.at[t, j, n], recv_sem=w_recv.at[t, j, n],
            device_id=dev, device_id_type=MESH,
        )

    def blk(t, j, y_, z_):
        return W.at[t, j, y_, z_, c]

    def pair(t, j, y_, c_):
        return W.at[t, j, y_, :, c_]

    def half(t, j, y_, h):
        return W.at[t, j, y_, zl, c, pl.ds(128 * h, 128)]

    def from_hbm(t, j, n, dev):
        w = (kw_hbm, vw_hbm)[t]
        return pltpu.make_async_remote_copy(
            src_ref=w.at[0, :, pl.ds(pl.multiple_of(j * CHUNK, CHUNK), CHUNK)], dst_ref=blk(t, j, y, zl),
            send_sem=w_send.at[t, j, n], recv_sem=w_recv.at[t, j, n], device_id=dev, device_id_type=MESH,
        )

    def own_copy(t, j):
        w = (kw_hbm, vw_hbm)[t]
        return pltpu.make_async_copy(
            w.at[0, :, pl.ds(pl.multiple_of(j * CHUNK, CHUNK), CHUNK)], blk(t, j, y, zl), own_sem.at[t, j]
        )

    def out(t, j, n, zf):
        if n == 0:
            return from_hbm(t, j, n, ZM)
        if n in (1, 2):
            dev = UP if n == 1 else DN
            return rcopy(t, j, n, dev, pair(t, j, y, c)) if zf else from_hbm(t, j, n, dev)
        if n == 3:
            return rcopy(t, j, n, UP, blk(t, j, ym, 0) if zf else half(t, j, ym, 0))
        if n == 4:
            return rcopy(t, j, n, DN, blk(t, j, yp, 1) if zf else half(t, j, yp, 1))
        if n <= 8:
            return rcopy(t, j, n, CM, pair(t, j, (y, ym, yp, yo)[n - 5], c))
        return rcopy(t, j, n, ZM, blk(t, j, (ym, yp, yo)[n - 9], zl))

    def inc(t, j, n, zf):
        if n == 0:
            return rcopy(t, j, n, ZM, blk(t, j, y, 1 - zl))
        if n in (1, 2):
            y_ = ym if n == 1 else yp
            return rcopy(t, j, n, DN if n == 1 else UP, pair(t, j, y_, c) if zf else blk(t, j, y_, zl))
        if n == 3:
            return rcopy(t, j, n, DN, blk(t, j, yo, 0) if zf else half(t, j, yo, 0))
        if n == 4:
            return rcopy(t, j, n, UP, blk(t, j, yo, 1) if zf else half(t, j, yo, 1))
        if n <= 8:
            return rcopy(t, j, n, CM, pair(t, j, (y, ym, yp, yo)[n - 5], 1 - c))
        return rcopy(t, j, n, ZM, blk(t, j, (ym, yp, yo)[n - 9], 1 - zl))

    def go(t, j, zf, *ns):
        for n in ns:
            out(t, j, n, zf).start()

    def wt(t, j, zf, *ns):
        for n in ns:
            inc(t, j, n, zf).wait_recv()

    def st1(t, j, zf):
        if zf:
            go(t, j, zf, 0)
        else:
            go(t, j, zf, 1, 2, 0)

    def st2(t, j, zf):
        own_copy(t, j).wait()
        if zf:
            wt(t, j, zf, 0)
            go(t, j, zf, 1, 2, 5)
        else:
            wt(t, j, zf, 1, 2)
            go(t, j, zf, 3, 4, 9, 10)
            wt(t, j, zf, 0)
            go(t, j, zf, 5)

    def st3(t, j, zf):
        if zf:
            wt(t, j, zf, 1, 2)
            go(t, j, zf, 3, 4, 6, 7)
        else:
            wt(t, j, zf, 3, 4)
            go(t, j, zf, 11)
            wt(t, j, zf, 9, 10)
            go(t, j, zf, 6, 7)

    def st4(t, j, zf):
        wt(t, j, zf, *((3, 4) if zf else (11,)))
        go(t, j, zf, 8)

    def st5(t, j, zf):
        wt(t, j, zf, 5, 6, 7, 8)

    def sent(t, j, zf):
        for n in range(9 if zf else 12):
            out(t, j, n, zf).wait_send()

    def routed(fn, j):
        fn(0, j, True)

        @pl.when(j == V_ZFIRST)
        def _():
            fn(1, j, True)

        @pl.when(j != V_ZFIRST)
        def _():
            fn(1, j, False)

    def first():
        for copy in local:
            copy.wait()
        for n in range(1, 7):
            enc_in(n).wait_recv()
        for t in range(2):
            low[t] = dot_nt(E[...], down[t]).astype(BF16)
            lowg[t] = jnp.zeros(lowg.shape[1:], F32)

    def compute(j):
        cols = pl.ds(pl.multiple_of(j * CHUNK, CHUNK), CHUNK)
        rows = []
        for t in range(2):
            weight = W[t, j].reshape(16 * BLOCK, CHUNK)
            base = jnp.dot(E[...], weight, preferred_element_type=F32)
            base = base + adapter_scale * jnp.dot(low[t], up[t, :, cols], preferred_element_type=F32)
            rows.append(base.astype(BF16))
        key_rows, value_rows = rows
        q, g = Q[:, cols], G[:, cols]
        lane = lax.broadcasted_iota(jnp.int32, (1, CHUNK), 1) // HEAD_DIM
        visible = lax.broadcasted_iota(jnp.int32, (BLOCK, 1), 0) < len_ref[0]
        dkeys = jnp.zeros((BLOCK, CHUNK), F32)
        dvalues = jnp.zeros((BLOCK, CHUNK), F32)
        zero = jnp.zeros((), BF16)
        for h in range(CHUNK // HEAD_DIM):
            here = lane == h
            scores = dot_nt(jnp.where(here, key_rows, zero), q)
            scores = jnp.where(visible, scores, masked_score)
            expo = jnp.exp(scores - jnp.max(scores, axis=0, keepdims=True))
            probs = (expo * (1.0 / jnp.sum(expo, axis=0, keepdims=True))).astype(BF16)
            dprobs = dot_nt(jnp.where(here, value_rows, zero), g)
            wide = probs.astype(F32)
            inner = jnp.sum(wide * dprobs, axis=0, keepdims=True)
            dscores = (wide * (dprobs - inner)).astype(BF16)
            dvalues = jnp.where(here, jnp.dot(probs, g, preferred_element_type=F32), dvalues)
            dkeys = jnp.where(here, jnp.dot(dscores, q, preferred_element_type=F32), dkeys)
        for t, grad in enumerate((dkeys, dvalues)):
            grad = grad.astype(BF16)
            dkv[t, j] = grad
            lowg[t] += dot_nt(grad, up[t, :, cols])
            up_grad = adapter_scale * dot_tn(low[t], grad)
            for half_ in range(2):
                A[2 * j + half_, pl.ds(16 * t, 16), 256:384] = up_grad[:, 128 * half_ : 128 * half_ + 128].astype(BF16)

    def slot(k, carry):
        for i, fn in enumerate((st1, st2, st3, st4, st5)):
            j = k - i

            @pl.when(jnp.logical_and(j >= 0, j < chunks))
            def _(fn=fn, j=j):
                routed(fn, j)

        @pl.when(k == 0)
        def _():
            enc_in(0).wait_recv()
            for n in range(4, 7):
                enc_out(n).start()

        @pl.when(k == 4)
        def _():
            first()

        @pl.when(k >= 4)
        def _():
            compute(k - 4)

        return carry

    lax.fori_loop(0, chunks + 4, slot, 0)

    for t in range(2):
        low[t] = (adapter_scale * lowg[t]).astype(BF16)

    def down_grad(r, carry):
        e = E[:, pl.ds(pl.multiple_of(r * BLOCK, BLOCK), BLOCK)]
        for t in range(2):
            A[r, pl.ds(16 * t, 16), 0:256] = dot_tn(low[t], e).astype(BF16)
        return carry

    lax.fori_loop(0, 16, down_grad, 0)

    def reduce_copy(o):
        return pltpu.make_async_remote_copy(
            src_ref=A.at[dp_peer(o)], dst_ref=A_recv.at[o], send_sem=r_send.at[o], recv_sem=r_recv.at[o],
            device_id=(dp_peer(o), sec), device_id_type=MESH,
        )

    for o in range(1, 16):
        reduce_copy(o).start()

    def partial_copy(i):
        return pltpu.make_async_remote_copy(
            src_ref=stage.at[i], dst_ref=out_recv.at[i], send_sem=o_send.at[i], recv_sem=o_recv.at[i],
            device_id=(dp, sec_at(i % 4 + 1, False)), device_id_type=MESH,
        )

    def cross_copy():
        return pltpu.make_async_remote_copy(
            src_ref=cross, dst_ref=cross_recv, send_sem=o_send.at[3], recv_sem=o_recv.at[3],
            device_id=(dp, sec_at(0, True)), device_id_type=MESH,
        )

    def back(i, carry):
        other = i < 4
        p = lax.rem(x + lax.rem(i, 4) + 1, 4) * 2 + jnp.where(other, 1 - zh, zh)
        for b in range(2):
            r = 2 * p + b
            r_y, r_z, r_c = r // 4, lax.rem(r // 2, 2), lax.rem(r, 2)
            acc = jnp.zeros((BLOCK, BLOCK), F32)
            for t in range(2):
                wide = jnp.concatenate([W[t, j, r_y, r_z, r_c] for j in range(chunks)], axis=1)
                grad = jnp.concatenate([dkv[t, j] for j in range(chunks)], axis=1)
                acc = acc + dot_nt(grad, wide)
                d = down[t, :, pl.ds(pl.multiple_of(r * BLOCK, BLOCK), BLOCK)]
                acc = acc + jnp.dot(low[t], d, preferred_element_type=F32)
            stage[i, :, b * BLOCK : (b + 1) * BLOCK] = acc.astype(BF16)

        for n in (0, 1, 2, 4, 5, 6):

            @pl.when(i == n)
            def _(n=n):
                partial_copy(n).start()

        return carry

    lax.fori_loop(0, 8, back, 0)

    total = A[dp].astype(F32)
    for o in range(1, 16):
        reduce_copy(o).wait_recv()
        total = total + A_recv[o].astype(F32)
    A_all[dp] = total

    def spread_copy(o, index):
        return pltpu.make_async_remote_copy(
            src_ref=A_all.at[index], dst_ref=A_all.at[index], send_sem=a_send.at[o], recv_sem=a_recv.at[o],
            device_id=(dp_peer(o), sec), device_id_type=MESH,
        )

    for o in range(1, 16):
        spread_copy(o, dp).start()

    def summed(first_, own_):
        total_ = stage[own_].astype(F32)
        for n in range(first_, first_ + 3):
            partial_copy(n).wait_recv()
            total_ = total_ + out_recv[n].astype(F32)
        return total_

    cross[...] = summed(0, 3).astype(BF16)
    cross_copy().start()

    for o in range(1, 16):
        r = lax.rem(dp + 16 - o, 16)
        spread_copy(o, r).wait_recv()
    for r in range(16):
        kd_ref[:, r * 256 : r * 256 + 256] = A_all[r, 0:16, 0:256]
        vd_ref[:, r * 256 : r * 256 + 256] = A_all[r, 16:32, 0:256]
        ku_ref[:, r * 128 : r * 128 + 128] = A_all[r, 0:16, 256:384]
        vu_ref[:, r * 128 : r * 128 + 128] = A_all[r, 16:32, 256:384]

    whole = summed(4, 7)
    cross_copy().wait_recv()
    out_ref[...] = (whole + cross_recv[...].astype(F32)).astype(BF16)

    def drain(j, carry):
        routed(sent, j)
        return carry

    lax.fori_loop(0, chunks, drain, 0)
    for n in range(7):
        enc_out(n).wait_send()
    for n in (0, 1, 2, 4, 5, 6):
        partial_copy(n).wait_send()
    cross_copy().wait_send()
    for o in range(1, 16):
        reduce_copy(o).wait_send()
        spread_copy(o, dp).wait_send()


def settle(*refs):
    sem = refs[-1]
    copies = [pltpu.make_async_copy(refs[i], refs[5 + i], sem.at[i]) for i in range(5)]
    for copy in copies:
        copy.start()
    for copy in copies:
        copy.wait()


def per_device(
    enc_states, queries, cotangent, enc_lengths, key_weight, value_weight, key_down, key_up, value_down, value_up
):
    inner = queries.shape[2]
    chunks = inner // CHUNK
    width = key_down.shape[1]
    columns = enc_states.shape[1]
    hbm = pl.BlockSpec(memory_space=pl.ANY)
    vmem = pl.BlockSpec(memory_space=pltpu.VMEM)
    dma = pltpu.SemaphoreType.DMA
    results = pl.pallas_call(
        functools.partial(kernel, chunks),
        out_shape=(
            jax.ShapeDtypeStruct((BLOCK, columns), BF16),
            jax.ShapeDtypeStruct((16, width), F32),
            jax.ShapeDtypeStruct((16, inner), F32),
            jax.ShapeDtypeStruct((16, width), F32),
            jax.ShapeDtypeStruct((16, inner), F32),
        ),
        in_specs=[hbm, hbm, hbm, pl.BlockSpec(memory_space=pltpu.SMEM)] + [hbm] * 6,
        out_specs=(vmem,) * 5,
        scratch_shapes=[
            pltpu.VMEM((2, chunks, 4, 2, 2, BLOCK, CHUNK), BF16),
            pltpu.VMEM((BLOCK, width), BF16),
            pltpu.VMEM(queries.shape[1:], BF16),
            pltpu.VMEM(cotangent.shape[1:], BF16),
            pltpu.VMEM((2, 16, width), BF16),
            pltpu.VMEM((2, 16, inner), BF16),
            pltpu.VMEM((2, BLOCK, 16), BF16),
            pltpu.VMEM((2, BLOCK, 16), F32),
            pltpu.VMEM((2, chunks, BLOCK, CHUNK), BF16),
            pltpu.VMEM((8, BLOCK, columns), BF16),
            pltpu.VMEM((8, BLOCK, columns), BF16),
            pltpu.VMEM((BLOCK, columns), BF16),
            pltpu.VMEM((BLOCK, columns), BF16),
            pltpu.VMEM((16, 32, 384), BF16),
            pltpu.VMEM((16, 32, 384), BF16),
            pltpu.VMEM((16, 32, 384), F32),
            dma((7,)),
            dma((2, chunks)),
            dma((2, chunks, 12)),
            dma((2, chunks, 12)),
            dma((8,)),
            dma((8,)),
            dma((8,)),
            dma((8,)),
            dma((16,)),
            dma((16,)),
            dma((16,)),
            dma((16,)),
        ],
        compiler_params=pltpu.CompilerParams(
            collective_id=0, has_side_effects=True, vmem_limit_bytes=60 * 1024 * 1024
        ),
        name="adapter_backward",
    )(
        enc_states, queries, cotangent, enc_lengths, key_weight, value_weight,
        key_down[0].T, key_up, value_down[0].T, value_up,
    )
    out, kd_grad, ku_grad, vd_grad, vu_grad = pl.pallas_call(
        settle,
        out_shape=tuple(jax.ShapeDtypeStruct(r.shape, r.dtype) for r in results),
        in_specs=[vmem] * 5,
        out_specs=(hbm,) * 5,
        scratch_shapes=[dma((5,))],
        name="results",
    )(*results)
    return out, kd_grad.T[None], ku_grad[None], vd_grad.T[None], vu_grad[None]


def solution(mesh):
    return jax.shard_map(
        per_device,
        mesh=mesh,
        in_specs=(
            P("dp", "section"),
            P("section", "dp", None),
            P("section", "dp", None),
            P("dp"),
            P("section", "dp", None),
            P("section", "dp", None),
            P("section", None, None),
            P("section", None, None),
            P("section", None, None),
            P("section", None, None),
        ),
        out_specs=(
            P("dp", "section"),
            P("section", None, None),
            P("section", None, None),
            P("section", None, None),
            P("section", None, None),
        ),
        check_vma=False,
    )
```

```python
import functools

import jax
import jax.numpy as jnp
from jax import lax
from jax.experimental import pallas as pl
from jax.experimental.pallas import tpu as pltpu
from jax.sharding import PartitionSpec as P

HEAD_DIM = 64
MESH = pl.DeviceIdType.MESH
adapter_scale = 0.5
masked_score = -1e30
F32 = jnp.float32
BF16 = jnp.bfloat16

FEATURES = 128
PACK = 2 * FEATURES
BLOCK = 256

NT = (((1,), (1,)), ((), ()))


def dot(a, b):
    return jnp.dot(a, b, preferred_element_type=F32)


def dot_nt(a, b):
    return lax.dot_general(a, b, NT, preferred_element_type=F32)


def kernel(
    chunks,
    enc_hbm, q_hbm, g_hbm, len_ref, kw_hbm, vw_hbm, kd_hbm, ku_hbm, vd_hbm, vu_hbm,
    out_ref, kd_ref, ku_ref, vd_ref, vu_ref,
    W, E, QG, lens, down, up, up_pack, low, low_t, lowg, dkv,
    stage, x_part, z_first, z_first_sum, z_sum, z_part, x_far,
    A, A_recv, A_all,
    local_sem, own_sem, q_own_sem, w_send, w_recv, q_send, q_recv,
    ez_send, ez_recv, ex_send, ex_recv, ef_send, ef_recv, len_send, len_recv,
    zf_send, zf_recv, xp_send, xp_recv, zp_send, zp_recv, far_send, far_recv,
    r_send, r_recv, a_send, a_recv,
):
    dp = lax.axis_index("dp")
    sec = lax.axis_index("section")
    c, zl, y = lax.rem(dp, 2), lax.rem(dp // 2, 2), dp // 4
    x, zh = sec // 2, lax.rem(sec, 2)
    yp, ym, yo = lax.rem(y + 1, 4), lax.rem(y + 3, 4), lax.rem(y + 2, 4)
    half = chunks * FEATURES
    columns = enc_hbm.shape[1]

    def did(y_, z_, c_):
        return ((y_ * 2 + z_) * 2 + c_, sec)

    UP, DN, ZM, CM = did(yp, zl, c), did(ym, zl, c), did(y, 1 - zl, c), did(y, zl, 1 - c)

    def dp_peer(o):
        return lax.rem(dp + o, 16)

    def sec_of(dx, zh_):
        return lax.rem(x + dx, 4) * 2 + zh_

    def x_peer(dx):
        return (dp, sec_of(dx, zh))

    z_coords = ((1 - zl, zh), (zl, 1 - zh), (1 - zl, 1 - zh))

    def z_peer(a):
        z_, h_ = z_coords[a]
        return ((y * 2 + z_) * 2 + c, x * 2 + h_)

    def remote(src, dst, send, recv, dev):
        return pltpu.make_async_remote_copy(
            src_ref=src, dst_ref=dst, send_sem=send, recv_sem=recv, device_id=dev, device_id_type=MESH
        )

    barrier = pltpu.get_barrier_semaphore()
    for o in range(1, 16):
        pl.semaphore_signal(barrier, inc=1, device_id=(dp_peer(o), sec), device_id_type=MESH)
    for dev in (x_peer(1), x_peer(2), x_peer(3), z_peer(1), z_peer(2)):
        pl.semaphore_signal(barrier, inc=1, device_id=dev, device_id_type=MESH)

    def section_columns(p):
        return pl.ds(pl.multiple_of(p * columns, columns), columns)

    def features(side, j):
        return pl.ds(pl.multiple_of(side * half + j * FEATURES, FEATURES), FEATURES)

    def lanes(t):
        return pl.ds(t * FEATURES, FEATURES)

    def own_copy(j, t):
        w = (kw_hbm, vw_hbm)[t]
        return pltpu.make_async_copy(w.at[0, :, features(zl, j)], W.at[j, y, zl, c, :, lanes(t)], own_sem.at[j, t])

    def q_own(j, t):
        q = (q_hbm, g_hbm)[t]
        return pltpu.make_async_copy(q.at[0, :, features(zl, j)], QG.at[j, zl, :, lanes(t)], q_own_sem.at[j, t])

    up_columns = pl.ds(pl.multiple_of(zl * half, half), half)
    local = [
        pltpu.make_async_copy(enc_hbm, E.at[zl, :, section_columns(sec)], local_sem.at[0]),
        pltpu.make_async_copy(kd_hbm, down.at[0:16], local_sem.at[1]),
        pltpu.make_async_copy(vd_hbm, down.at[16:32], local_sem.at[2]),
        pltpu.make_async_copy(ku_hbm.at[0, :, up_columns], up.at[0], local_sem.at[3]),
        pltpu.make_async_copy(vu_hbm.at[0, :, up_columns], up.at[1], local_sem.at[4]),
    ]
    for j in range(chunks):
        for t in range(2):
            own_copy(j, t).start()
    for copy in local:
        copy.start()
    for j in range(chunks):
        for t in range(2):
            q_own(j, t).start()
    lens[zl] = jnp.full(lens.shape[1:], len_ref[0], jnp.int32)
    A[...] = jnp.zeros(A.shape, BF16)
    pl.semaphore_wait(barrier, 20)

    def pair(j, y_, c_):
        return W.at[j, y_, :, c_]

    def w_copy(j, n, dev, ref):
        return remote(ref, ref, w_send.at[j, n], w_recv.at[j, n], dev)

    def w_out(j, n):
        if n in (0, 9):
            t = 0 if n == 0 else 1
            w = (kw_hbm, vw_hbm)[t]
            return remote(
                w.at[0, :, features(1 - zl, j)], W.at[j, y, zl, c, :, lanes(t)], w_send.at[j, n], w_recv.at[j, n], ZM
            )
        if n in (1, 2):
            return w_copy(j, n, UP if n == 1 else DN, pair(j, y, c))
        if n == 3:
            return w_copy(j, n, UP, W.at[j, ym, 0, c])
        if n == 4:
            return w_copy(j, n, DN, W.at[j, yp, 1, c])
        return w_copy(j, n, CM, pair(j, (y, ym, yp, yo)[n - 5], c))

    def w_in(j, n):
        if n in (0, 9):
            return w_copy(j, n, ZM, W.at[j, y, 1 - zl, c, :, lanes(0 if n == 0 else 1)])
        if n in (1, 2):
            return w_copy(j, n, DN if n == 1 else UP, pair(j, ym if n == 1 else yp, c))
        if n in (3, 4):
            return w_copy(j, n, DN if n == 3 else UP, W.at[j, yo, n - 3, c])
        return w_copy(j, n, CM, pair(j, (y, ym, yp, yo)[n - 5], 1 - c))

    def go(j, *ns):
        for n in ns:
            w_out(j, n).start()

    def wt(j, *ns):
        for n in ns:
            w_in(j, n).wait_recv()

    def st1(j):
        go(j, 0, 9)

    def st2(j):
        for t in range(2):
            own_copy(j, t).wait()
        wt(j, 0, 9)
        go(j, 1, 2, 5)

    def st3(j):
        wt(j, 1, 2)
        go(j, 3, 4, 6, 7)

    def st4(j):
        wt(j, 3, 4)
        go(j, 8)

    def st5(j):
        wt(j, 5, 6, 7, 8)

    def q_out(j, t):
        q = (q_hbm, g_hbm)[t]
        return remote(
            q.at[0, :, features(1 - zl, j)], QG.at[j, zl, :, lanes(t)], q_send.at[j, t], q_recv.at[j, t], ZM
        )

    def q_in(j, t):
        ref = QG.at[j, 1 - zl, :, lanes(t)]
        return remote(ref, ref, q_send.at[j, t], q_recv.at[j, t], ZM)

    def send_q(j):
        for t in range(2):
            q_out(j, t).start()

    def e_piece(s, p):
        return E.at[s, :, section_columns(p)]

    def ez_out(a):
        return remote(enc_hbm, e_piece(zl, sec), ez_send.at[a], ez_recv.at[a], z_peer(a))

    def ez_in(a):
        z_, h_ = z_coords[a]
        ref = e_piece(z_, x * 2 + h_)
        return remote(ref, ref, ez_send.at[a], ez_recv.at[a], z_peer(a))

    def ex_out(d, k):
        dev = x_peer(1 if d == 0 else 3)
        if k == 0:
            return remote(enc_hbm, e_piece(zl, sec), ex_send.at[d, k], ex_recv.at[d, k], dev)
        z_, h_ = z_coords[k - 1]
        ref = e_piece(z_, x * 2 + h_)
        return remote(ref, ref, ex_send.at[d, k], ex_recv.at[d, k], dev)

    def ex_in(d, m, s):
        k = 2 * m + jnp.where(s == zl, 0, 1)
        ref = e_piece(s, sec_of(3 if d == 0 else 1, 1 - zh if m else zh))
        return remote(ref, ref, ex_send.at[d, k], ex_recv.at[d, k], x_peer(3 if d == 0 else 1))

    def ef_out(d, m):
        ref = e_piece(d, sec_of(3 if d == 0 else 1, 1 - zh if m else zh))
        return remote(ref, ref, ef_send.at[d, m], ef_recv.at[d, m], x_peer(1 if d == 0 else 3))

    def ef_in(d, m):
        ref = e_piece(d, sec_of(2, 1 - zh if m else zh))
        return remote(ref, ref, ef_send.at[d, m], ef_recv.at[d, m], x_peer(3 if d == 0 else 1))

    def e_second():
        for a in range(3):
            ez_in(a).wait_recv()
            for d in range(2):
                ex_out(d, a + 1).start()

    def e_third():
        for m in range(2):
            for d in range(2):
                ex_in(d, m, d).wait_recv()
                ef_out(d, m).start()

    def len_copy(s):
        return remote(lens.at[s], lens.at[s], len_send.at[0], len_recv.at[0], ZM)

    st1(0)
    for a in range(3):
        ez_out(a).start()
    for d in range(2):
        ex_out(d, 0).start()
    len_copy(zl).start()

    def first():
        for copy in local:
            copy.wait()
        len_copy(1 - zl).wait_recv()
        for m in range(2):
            for d in range(2):
                ex_in(d, m, 1 - d).wait_recv()
                ef_in(d, m).wait_recv()
        states = E[...].reshape(2 * BLOCK, E.shape[2])
        low[...] = dot_nt(states, down[...]).astype(BF16)
        low_t[...] = dot_nt(down[...], states).astype(BF16)
        lowg[...] = jnp.zeros(lowg.shape, F32)
        up_pack[...] = jnp.zeros(up_pack.shape, BF16)
        for j in range(chunks):
            for t in range(2):
                up_pack[j, 16 * t : 16 * t + 16, FEATURES * t : FEATURES * t + FEATURES] = up[
                    t, :, FEATURES * j : FEATURES * j + FEATURES
                ]

    def compute(j):
        for t in range(2):
            q_own(j, t).wait()
            q_in(j, t).wait_recv()
        weight = W[j].reshape(16 * BLOCK, PACK)
        base = dot(E[...].reshape(2 * BLOCK, E.shape[2]), weight)
        base = base + adapter_scale * dot(low[...], up_pack[j])
        rows = base.astype(BF16)
        lane = lax.broadcasted_iota(jnp.int32, (1, FEATURES), 1) // HEAD_DIM
        index = lax.broadcasted_iota(jnp.int32, (BLOCK, 1), 0)
        zero = jnp.zeros((), BF16)
        grads = []
        for s in range(2):
            visible = index < lens[s, 0:1, 0:1]
            key_rows = rows[BLOCK * s : BLOCK * s + BLOCK, :FEATURES]
            value_rows = rows[BLOCK * s : BLOCK * s + BLOCK, FEATURES:]
            q, g = QG[j, s, :, :FEATURES], QG[j, s, :, FEATURES:]
            dkeys = jnp.zeros((BLOCK, FEATURES), F32)
            dvalues = jnp.zeros((BLOCK, FEATURES), F32)
            for h in range(FEATURES // HEAD_DIM):
                here = lane == h
                scores = dot_nt(jnp.where(here, key_rows, zero), q)
                scores = jnp.where(visible, scores, masked_score)
                expo = jnp.exp(scores - jnp.max(scores, axis=0, keepdims=True))
                probs = (expo * (1.0 / jnp.sum(expo, axis=0, keepdims=True))).astype(BF16)
                dprobs = dot_nt(jnp.where(here, value_rows, zero), g)
                wide = probs.astype(F32)
                inner = jnp.sum(wide * dprobs, axis=0, keepdims=True)
                dscores = (wide * (dprobs - inner)).astype(BF16)
                dvalues = jnp.where(here, dot(probs, g), dvalues)
                dkeys = jnp.where(here, dot(dscores, q), dkeys)
            grads.append(jnp.concatenate([dkeys, dvalues], axis=1).astype(BF16))
        grad = jnp.concatenate(grads, axis=0)
        dkv[:, pl.ds(pl.multiple_of(j * PACK, PACK), PACK)] = grad
        lowg[...] += dot_nt(grad, up_pack[j])
        up_grad = adapter_scale * dot(low_t[...], grad)
        r = ((j // 2) * 2 + zl) * 2 + lax.rem(j, 2)
        for t in range(2):
            A[r, pl.ds(16 * t, 16), 256:384] = up_grad[
                16 * t : 16 * t + 16, FEATURES * t : FEATURES * t + FEATURES
            ].astype(BF16)

    def within(j, fn):
        @pl.when(jnp.logical_and(j >= 0, j < chunks))
        def _():
            fn(j)

    def slot(k, carry):
        within(k + 1, st1)
        within(k, st2)

        @pl.when(k == 0)
        def _():
            e_second()

        within(k - 1, send_q)
        within(k - 1, st3)

        @pl.when(k == 3)
        def _():
            e_third()

        within(k - 2, st4)
        within(k - 3, st5)

        @pl.when(k == 3)
        def _():
            first()

        within(k - 3, compute)
        return carry

    lax.fori_loop(0, chunks + 3, slot, 0)

    scaled = adapter_scale * lowg[...]
    low[...] = scaled.astype(BF16)
    both = scaled.T.astype(BF16)

    def down_grad(r, carry):
        e = E[:, :, pl.ds(pl.multiple_of(r * BLOCK, BLOCK), BLOCK)].reshape(2 * BLOCK, BLOCK)
        A[r, :, 0:256] = dot(both, e).astype(BF16)
        return carry

    lax.fori_loop(0, 16, down_grad, 0, unroll=4)

    def reduce_copy(o):
        return remote(A.at[dp_peer(o)], A_recv.at[o], r_send.at[o], r_recv.at[o], (dp_peer(o), sec))

    for o in range(1, 16):
        reduce_copy(o).start()

    def back_place(i):
        dx = jnp.where(i < 2, 2, jnp.where(i < 6, 1 + 2 * lax.rem(i, 2), 0))
        other = jnp.where(i < 2, 1 - i, jnp.where(i < 6, 1 - (i - 2) // 2, 7 - i))
        return dx, other

    def z_first_copy(a):
        s = z_coords[a][0]
        i = 1 if a == 0 else 0
        return remote(stage.at[i, s], z_first.at[a], zf_send.at[a], zf_recv.at[a], z_peer(a))

    def x_part_copy(d, e, s):
        i = (4 if e == 0 else 2) + d
        return remote(stage.at[i, s], x_part.at[d, e, s], xp_send.at[d, e, s], xp_recv.at[d, e, s], x_peer(1 if d == 0 else 3))

    def z_part_copy(a):
        return remote(z_sum.at[a], z_part.at[a], zp_send.at[a], zp_recv.at[a], z_peer(a))

    def far_copy():
        return remote(z_first_sum, x_far, far_send.at[0], far_recv.at[0], x_peer(2))

    def back(i, carry):
        dx, other = back_place(i)
        p = lax.rem(x + dx, 4) * 2 + jnp.where(other == 1, 1 - zh, zh)
        for b in range(2):
            r = 2 * p + b
            r_y, r_z, r_c = r // 4, lax.rem(r // 2, 2), lax.rem(r, 2)
            wide = jnp.concatenate([W[j, r_y, r_z, r_c] for j in range(chunks)], axis=1)
            acc = dot_nt(dkv[...], wide)
            acc = acc + dot(low[...], down[:, pl.ds(pl.multiple_of(r * BLOCK, BLOCK), BLOCK)])
            stage[i, :, :, b * BLOCK : (b + 1) * BLOCK] = acc.astype(BF16).reshape(2, BLOCK, BLOCK)

        @pl.when(i == 0)
        def _():
            z_first_copy(2).start()
            z_first_copy(1).start()

        @pl.when(i == 1)
        def _():
            z_first_copy(0).start()

        for d in range(2):
            for e in range(2):

                @pl.when(i == (4 if e == 0 else 2) + d)
                def _(d=d, e=e):
                    x_part_copy(d, e, 1 - zl).start()
                    x_part_copy(d, e, zl).start()

        return carry

    lax.fori_loop(0, 8, back, 0)

    total = stage[1, zl].astype(F32)
    for a in range(3):
        z_first_copy(a).wait_recv()
        total = total + z_first[a].astype(F32)
    z_first_sum[...] = total.astype(BF16)
    far_copy().start()

    def drain(j, carry):
        for n in range(10):
            w_out(j, n).wait_send()
        for t in range(2):
            q_out(j, t).wait_send()
        return carry

    lax.fori_loop(0, chunks, drain, 0)
    for a in range(3):
        ez_out(a).wait_send()
    for d in range(2):
        for k in range(4):
            ex_out(d, k).wait_send()
        for m in range(2):
            ef_out(d, m).wait_send()
    len_copy(zl).wait_send()

    total = A[dp].astype(F32)
    for o in range(1, 16):
        reduce_copy(o).wait_recv()
        total = total + A_recv[o].astype(F32)
    A_all[dp] = total

    def spread_copy(o, index):
        return remote(A_all.at[index], A_all.at[index], a_send.at[o], a_recv.at[o], (dp_peer(o), sec))

    for o in range(1, 16):
        spread_copy(o, dp).start()

    def over_x(e, s):
        sum_ = stage[7 - e, s].astype(F32)
        for d in range(2):
            x_part_copy(d, e, s).wait_recv()
            sum_ = sum_ + x_part[d, e, s].astype(F32)
        return sum_

    for a in (2, 1, 0):
        z_sum[a] = over_x(0 if a == 0 else 1, z_coords[a][0]).astype(BF16)
        z_part_copy(a).start()

    for o in range(1, 16):
        spread_copy(o, lax.rem(dp + 16 - o, 16)).wait_recv()
    for r in range(16):
        first_up = r // 2 % 2 * half + (r // 4 * 2 + r % 2) * FEATURES
        kd_ref[:, r * 256 : r * 256 + 256] = A_all[r, 0:16, 0:256]
        vd_ref[:, r * 256 : r * 256 + 256] = A_all[r, 16:32, 0:256]
        ku_ref[:, pl.ds(first_up, FEATURES)] = A_all[r, 0:16, 256:384]
        vu_ref[:, pl.ds(first_up, FEATURES)] = A_all[r, 16:32, 256:384]

    total = over_x(0, zl)
    far_copy().wait_recv()
    total = total + x_far[...].astype(F32)
    for a in (2, 1, 0):
        z_part_copy(a).wait_recv()
        total = total + z_part[a].astype(F32)
    out_ref[...] = total.astype(BF16)

    for a in range(3):
        z_first_copy(a).wait_send()
        z_part_copy(a).wait_send()
    for d in range(2):
        for e in range(2):
            for s in range(2):
                x_part_copy(d, e, s).wait_send()
    far_copy().wait_send()
    for o in range(1, 16):
        reduce_copy(o).wait_send()
        spread_copy(o, dp).wait_send()


def settle(*refs):
    sem = refs[-1]
    copies = [pltpu.make_async_copy(refs[i], refs[5 + i], sem.at[i]) for i in range(5)]
    for copy in copies:
        copy.start()
    for copy in copies:
        copy.wait()


def per_device(
    enc_states, queries, cotangent, enc_lengths, key_weight, value_weight, key_down, key_up, value_down, value_up
):
    inner = queries.shape[2]
    chunks = inner // 2 // FEATURES
    width = key_down.shape[1]
    columns = enc_states.shape[1]
    rows = queries.shape[1]
    hbm = pl.BlockSpec(memory_space=pl.ANY)
    vmem = pl.BlockSpec(memory_space=pltpu.VMEM)
    dma = pltpu.SemaphoreType.DMA
    piece = (BLOCK, columns)
    results = pl.pallas_call(
        functools.partial(kernel, chunks),
        out_shape=(
            jax.ShapeDtypeStruct((BLOCK, columns), BF16),
            jax.ShapeDtypeStruct((16, width), F32),
            jax.ShapeDtypeStruct((16, inner), F32),
            jax.ShapeDtypeStruct((16, width), F32),
            jax.ShapeDtypeStruct((16, inner), F32),
        ),
        in_specs=[hbm, hbm, hbm, pl.BlockSpec(memory_space=pltpu.SMEM)] + [hbm] * 6,
        out_specs=(vmem,) * 5,
        scratch_shapes=[
            pltpu.VMEM((chunks, 4, 2, 2, BLOCK, PACK), BF16),
            pltpu.VMEM((2, BLOCK, width), BF16),
            pltpu.VMEM((chunks, 2, rows, PACK), BF16),
            pltpu.VMEM((2, 8, 128), jnp.int32),
            pltpu.VMEM((32, width), BF16),
            pltpu.VMEM((2, 16, inner // 2), BF16),
            pltpu.VMEM((chunks, 32, PACK), BF16),
            pltpu.VMEM((2 * BLOCK, 32), BF16),
            pltpu.VMEM((32, 2 * BLOCK), BF16),
            pltpu.VMEM((2 * BLOCK, 32), F32),
            pltpu.VMEM((2 * BLOCK, chunks * PACK), BF16),
            pltpu.VMEM((8, 2) + piece, BF16),
            pltpu.VMEM((2, 2, 2) + piece, BF16),
            pltpu.VMEM((3,) + piece, BF16),
            pltpu.VMEM(piece, BF16),
            pltpu.VMEM((3,) + piece, BF16),
            pltpu.VMEM((3,) + piece, BF16),
            pltpu.VMEM(piece, BF16),
            pltpu.VMEM((16, 32, 384), BF16),
            pltpu.VMEM((16, 32, 384), BF16),
            pltpu.VMEM((16, 32, 384), F32),
            dma((5,)),
            dma((chunks, 2)),
            dma((chunks, 2)),
            dma((chunks, 10)),
            dma((chunks, 10)),
            dma((chunks, 2)),
            dma((chunks, 2)),
            dma((3,)),
            dma((3,)),
            dma((2, 4)),
            dma((2, 4)),
            dma((2, 2)),
            dma((2, 2)),
            dma((1,)),
            dma((1,)),
            dma((3,)),
            dma((3,)),
            dma((2, 2, 2)),
            dma((2, 2, 2)),
            dma((3,)),
            dma((3,)),
            dma((1,)),
            dma((1,)),
            dma((16,)),
            dma((16,)),
            dma((16,)),
            dma((16,)),
        ],
        compiler_params=pltpu.CompilerParams(
            collective_id=0, has_side_effects=True, vmem_limit_bytes=60 * 1024 * 1024
        ),
        name="adapter_backward",
    )(
        enc_states, queries, cotangent, enc_lengths, key_weight, value_weight,
        key_down[0].T, key_up, value_down[0].T, value_up,
    )
    out, kd_grad, ku_grad, vd_grad, vu_grad = pl.pallas_call(
        settle,
        out_shape=tuple(jax.ShapeDtypeStruct(r.shape, r.dtype) for r in results),
        in_specs=[vmem] * 5,
        out_specs=(hbm,) * 5,
        scratch_shapes=[dma((5,))],
        name="results",
    )(*results)
    return out, kd_grad.T[None], ku_grad[None], vd_grad.T[None], vu_grad[None]


def solution(mesh):
    return jax.shard_map(
        per_device,
        mesh=mesh,
        in_specs=(
            P("dp", "section"),
            P("section", "dp", None),
            P("section", "dp", None),
            P("dp"),
            P("section", "dp", None),
            P("section", "dp", None),
            P("section", None, None),
            P("section", None, None),
            P("section", None, None),
            P("section", None, None),
        ),
        out_specs=(
            P("dp", "section"),
            P("section", None, None),
            P("section", None, None),
            P("section", None, None),
            P("section", None, None),
        ),
        check_vma=False,
    )
```

```python
import functools

import jax
import jax.numpy as jnp
from jax import lax
from jax.experimental import pallas as pl
from jax.experimental.pallas import tpu as pltpu
from jax.sharding import PartitionSpec as P

HEAD_DIM = 64
MESH = pl.DeviceIdType.MESH
adapter_scale = 0.5
masked_score = -1e30
F32 = jnp.float32
BF16 = jnp.bfloat16

FEATURES = 128
PACK = 2 * FEATURES
BLOCK = 256

NT = (((1,), (1,)), ((), ()))


def dot(a, b):
    return jnp.dot(a, b, preferred_element_type=F32)


def dot_nt(a, b):
    return lax.dot_general(a, b, NT, preferred_element_type=F32)


def kernel(
    chunks,
    enc_hbm, q_hbm, g_hbm, len_ref, kw_hbm, vw_hbm, kd_hbm, ku_hbm, vd_hbm, vu_hbm,
    out_ref, kd_ref, ku_ref, vd_ref, vu_ref,
    W, E, QG, lens, down, up, up_pack, low, low_t, lowg, dkv,
    stage, x_part, z_first, z_first_sum, z_sum, z_part, x_far,
    A, A_core, A_sum, A_recv, A_all,
    local_sem, own_sem, q_own_sem, w_send, w_recv, q_send, q_recv,
    ez_send, ez_recv, ex_send, ex_recv, ef_send, ef_recv, len_send, len_recv,
    zf_send, zf_recv, xp_send, xp_recv, zp_send, zp_recv, far_send, far_recv,
    r_send, r_recv, a_send, a_recv,
):
    dp = lax.axis_index("dp")
    sec = lax.axis_index("section")
    c, zl, y = lax.rem(dp, 2), lax.rem(dp // 2, 2), dp // 4
    x, zh = sec // 2, lax.rem(sec, 2)
    yp, ym, yo = lax.rem(y + 1, 4), lax.rem(y + 3, 4), lax.rem(y + 2, 4)
    half = chunks * FEATURES
    columns = enc_hbm.shape[1]

    def did(y_, z_, c_):
        return ((y_ * 2 + z_) * 2 + c_, sec)

    UP, DN, ZM, CM = did(yp, zl, c), did(ym, zl, c), did(y, 1 - zl, c), did(y, zl, 1 - c)

    me = dp // 2

    def chip(o):
        return lax.rem(me + o, 8)

    def chip_device(o):
        return (chip(o) * 2 + c, sec)

    def sec_of(dx, zh_):
        return lax.rem(x + dx, 4) * 2 + zh_

    def x_peer(dx):
        return (dp, sec_of(dx, zh))

    z_coords = ((1 - zl, zh), (zl, 1 - zh), (1 - zl, 1 - zh))

    def z_peer(a):
        z_, h_ = z_coords[a]
        return ((y * 2 + z_) * 2 + c, x * 2 + h_)

    def remote(src, dst, send, recv, dev):
        return pltpu.make_async_remote_copy(
            src_ref=src, dst_ref=dst, send_sem=send, recv_sem=recv, device_id=dev, device_id_type=MESH
        )

    barrier = pltpu.get_barrier_semaphore()
    for o in range(1, 8):
        pl.semaphore_signal(barrier, inc=1, device_id=chip_device(o), device_id_type=MESH)
    for dev in (CM, x_peer(1), x_peer(2), x_peer(3), z_peer(1), z_peer(2)):
        pl.semaphore_signal(barrier, inc=1, device_id=dev, device_id_type=MESH)

    def section_columns(p):
        return pl.ds(pl.multiple_of(p * columns, columns), columns)

    def features(side, j):
        return pl.ds(pl.multiple_of(side * half + j * FEATURES, FEATURES), FEATURES)

    def lanes(t):
        return pl.ds(t * FEATURES, FEATURES)

    def own_copy(j, t):
        w = (kw_hbm, vw_hbm)[t]
        return pltpu.make_async_copy(w.at[0, :, features(zl, j)], W.at[j, y, zl, c, :, lanes(t)], own_sem.at[j, t])

    def q_own(j, t):
        q = (q_hbm, g_hbm)[t]
        return pltpu.make_async_copy(q.at[0, :, features(zl, j)], QG.at[j, zl, :, lanes(t)], q_own_sem.at[j, t])

    up_columns = pl.ds(pl.multiple_of(zl * half, half), half)
    local = [
        pltpu.make_async_copy(enc_hbm, E.at[zl, :, section_columns(sec)], local_sem.at[0]),
        pltpu.make_async_copy(kd_hbm, down.at[0:16], local_sem.at[1]),
        pltpu.make_async_copy(vd_hbm, down.at[16:32], local_sem.at[2]),
        pltpu.make_async_copy(ku_hbm.at[0, :, up_columns], up.at[0], local_sem.at[3]),
        pltpu.make_async_copy(vu_hbm.at[0, :, up_columns], up.at[1], local_sem.at[4]),
    ]
    for j in range(chunks):
        for t in range(2):
            own_copy(j, t).start()
    for copy in local:
        copy.start()
    for j in range(chunks):
        for t in range(2):
            q_own(j, t).start()
    lens[zl] = jnp.full(lens.shape[1:], len_ref[0], jnp.int32)
    A[...] = jnp.zeros(A.shape, BF16)
    pl.semaphore_wait(barrier, 13)

    def pair(j, y_, c_):
        return W.at[j, y_, :, c_]

    def w_copy(j, n, dev, ref):
        return remote(ref, ref, w_send.at[j, n], w_recv.at[j, n], dev)

    def w_out(j, n):
        if n in (0, 9):
            t = 0 if n == 0 else 1
            w = (kw_hbm, vw_hbm)[t]
            return remote(
                w.at[0, :, features(1 - zl, j)], W.at[j, y, zl, c, :, lanes(t)], w_send.at[j, n], w_recv.at[j, n], ZM
            )
        if n in (1, 2, 10, 11):
            t = 0 if n in (1, 2) else 1
            w = (kw_hbm, vw_hbm)[t]
            return remote(
                w.at[0, :, features(zl, j)], W.at[j, y, zl, c, :, lanes(t)], w_send.at[j, n], w_recv.at[j, n],
                UP if n in (1, 10) else DN,
            )
        if n in (12, 13):
            return w_copy(j, n, UP if n == 12 else DN, W.at[j, y, 1 - zl, c])
        if n == 3:
            return w_copy(j, n, UP, W.at[j, ym, 0, c])
        if n == 4:
            return w_copy(j, n, DN, W.at[j, yp, 1, c])
        return w_copy(j, n, CM, pair(j, (y, ym, yp, yo)[n - 5], c))

    def w_in(j, n):
        if n in (0, 9):
            return w_copy(j, n, ZM, W.at[j, y, 1 - zl, c, :, lanes(0 if n == 0 else 1)])
        if n in (1, 2, 10, 11):
            up_ = n in (1, 10)
            t = 0 if n in (1, 2) else 1
            return w_copy(j, n, DN if up_ else UP, W.at[j, ym if up_ else yp, zl, c, :, lanes(t)])
        if n in (12, 13):
            return w_copy(j, n, DN if n == 12 else UP, W.at[j, ym if n == 12 else yp, 1 - zl, c])
        if n in (3, 4):
            return w_copy(j, n, DN if n == 3 else UP, W.at[j, yo, n - 3, c])
        return w_copy(j, n, CM, pair(j, (y, ym, yp, yo)[n - 5], 1 - c))

    def go(j, *ns):
        for n in ns:
            w_out(j, n).start()

    def wt(j, *ns):
        for n in ns:
            w_in(j, n).wait_recv()

    def st1(j):
        go(j, 0, 9, 1, 2, 10, 11)

    def st2(j):
        for t in range(2):
            own_copy(j, t).wait()
        wt(j, 0, 9)
        go(j, 12, 13, 5)

    def st3(j):
        wt(j, 1, 2, 10, 11, 12, 13)
        go(j, 3, 4, 6, 7)

    def st4(j):
        wt(j, 3, 4)
        go(j, 8)

    def st5(j):
        wt(j, 5, 6, 7, 8)

    def q_out(j, t):
        q = (q_hbm, g_hbm)[t]
        return remote(
            q.at[0, :, features(1 - zl, j)], QG.at[j, zl, :, lanes(t)], q_send.at[j, t], q_recv.at[j, t], ZM
        )

    def q_in(j, t):
        ref = QG.at[j, 1 - zl, :, lanes(t)]
        return remote(ref, ref, q_send.at[j, t], q_recv.at[j, t], ZM)

    def send_q(j):
        for t in range(2):
            q_out(j, t).start()

    def e_piece(s, p):
        return E.at[s, :, section_columns(p)]

    def ez_out(a):
        return remote(enc_hbm, e_piece(zl, sec), ez_send.at[a], ez_recv.at[a], z_peer(a))

    def ez_in(a):
        z_, h_ = z_coords[a]
        ref = e_piece(z_, x * 2 + h_)
        return remote(ref, ref, ez_send.at[a], ez_recv.at[a], z_peer(a))

    def ex_out(d, k):
        dev = x_peer(1 if d == 0 else 3)
        if k == 0:
            return remote(enc_hbm, e_piece(zl, sec), ex_send.at[d, k], ex_recv.at[d, k], dev)
        z_, h_ = z_coords[k - 1]
        ref = e_piece(z_, x * 2 + h_)
        return remote(ref, ref, ex_send.at[d, k], ex_recv.at[d, k], dev)

    def ex_in(d, m, s):
        k = 2 * m + jnp.where(s == zl, 0, 1)
        ref = e_piece(s, sec_of(3 if d == 0 else 1, 1 - zh if m else zh))
        return remote(ref, ref, ex_send.at[d, k], ex_recv.at[d, k], x_peer(3 if d == 0 else 1))

    def ef_out(d, m):
        ref = e_piece(d, sec_of(3 if d == 0 else 1, 1 - zh if m else zh))
        return remote(ref, ref, ef_send.at[d, m], ef_recv.at[d, m], x_peer(1 if d == 0 else 3))

    def ef_in(d, m):
        ref = e_piece(d, sec_of(2, 1 - zh if m else zh))
        return remote(ref, ref, ef_send.at[d, m], ef_recv.at[d, m], x_peer(3 if d == 0 else 1))

    def e_second():
        for a in range(3):
            ez_in(a).wait_recv()
            for d in range(2):
                ex_out(d, a + 1).start()

    def e_third():
        for m in range(2):
            for d in range(2):
                ex_in(d, m, d).wait_recv()
                ef_out(d, m).start()

    def len_copy(s):
        return remote(lens.at[s], lens.at[s], len_send.at[0], len_recv.at[0], ZM)

    st1(0)
    st1(1)
    for a in range(3):
        ez_out(a).start()
    for d in range(2):
        ex_out(d, 0).start()
    len_copy(zl).start()

    def first():
        for copy in local:
            copy.wait()
        len_copy(1 - zl).wait_recv()
        for m in range(2):
            for d in range(2):
                ex_in(d, m, 1 - d).wait_recv()
                ef_in(d, m).wait_recv()
        states = E[...].reshape(2 * BLOCK, E.shape[2])
        low[...] = dot_nt(states, down[...]).astype(BF16)
        low_t[...] = dot_nt(down[...], states).astype(BF16)
        lowg[...] = jnp.zeros(lowg.shape, F32)
        up_pack[...] = jnp.zeros(up_pack.shape, BF16)
        for j in range(chunks):
            for t in range(2):
                up_pack[j, 16 * t : 16 * t + 16, FEATURES * t : FEATURES * t + FEATURES] = up[
                    t, :, FEATURES * j : FEATURES * j + FEATURES
                ]

    def compute(j):
        for t in range(2):
            q_own(j, t).wait()
            q_in(j, t).wait_recv()
        weight = W[j].reshape(16 * BLOCK, PACK)
        base = dot(E[...].reshape(2 * BLOCK, E.shape[2]), weight)
        base = base + adapter_scale * dot(low[...], up_pack[j])
        here_columns = pl.ds(pl.multiple_of(j * PACK, PACK), PACK)
        dkv[:, here_columns] = base.astype(BF16)
        lane = lax.broadcasted_iota(jnp.int32, (1, FEATURES), 1) // HEAD_DIM
        index = lax.broadcasted_iota(jnp.int32, (BLOCK, 1), 0)
        zero = jnp.zeros((), BF16)

        def sequence(s, carry):
            here_rows = pl.ds(pl.multiple_of(s * BLOCK, BLOCK), BLOCK)
            rows = dkv[here_rows, here_columns]
            key_rows, value_rows = rows[:, :FEATURES], rows[:, FEATURES:]
            q, g = QG[j, s, :, :FEATURES], QG[j, s, :, FEATURES:]
            visible = index < lens[s, 0:1, 0:1]
            scores = dot_nt(jnp.concatenate([jnp.where(lane == h, key_rows, zero) for h in range(2)], axis=0), q)
            dprobs = dot_nt(jnp.concatenate([jnp.where(lane == h, value_rows, zero) for h in range(2)], axis=0), g)
            all_probs, all_dscores = [], []
            for h in range(2):
                masked = jnp.where(visible, scores[BLOCK * h : BLOCK * h + BLOCK], masked_score)
                expo = jnp.exp(masked - jnp.max(masked, axis=0, keepdims=True))
                probs = (expo * (1.0 / jnp.sum(expo, axis=0, keepdims=True))).astype(BF16)
                wide = probs.astype(F32)
                dprob = dprobs[BLOCK * h : BLOCK * h + BLOCK]
                inner = jnp.sum(wide * dprob, axis=0, keepdims=True)
                all_probs.append(probs)
                all_dscores.append((wide * (dprob - inner)).astype(BF16))
            dvalues = dot(jnp.concatenate(all_probs, axis=0), g)
            dkeys = dot(jnp.concatenate(all_dscores, axis=0), q)
            both = [jnp.where(lane == 0, d[:BLOCK], d[BLOCK:]) for d in (dkeys, dvalues)]
            dkv[here_rows, here_columns] = jnp.concatenate(both, axis=1).astype(BF16)
            return carry

        lax.fori_loop(0, 2, sequence, 0)
        grad = dkv[:, here_columns]
        lowg[...] += dot_nt(grad, up_pack[j])
        up_grad = adapter_scale * dot(low_t[...], grad)
        r = (j // 2) * 2 + zl
        r_core = lax.rem(j, 2)
        for t in range(2):
            A[r, r_core, pl.ds(16 * t, 16), 256:384] = up_grad[
                16 * t : 16 * t + 16, FEATURES * t : FEATURES * t + FEATURES
            ].astype(BF16)

    def within(j, fn):
        @pl.when(jnp.logical_and(j >= 0, j < chunks))
        def _():
            fn(j)

    computed = (10, 12, 13, 14, 15, 17, 19, 21)

    def half_slot(i, carry):
        k = i // 2

        @pl.when(lax.rem(i, 2) == 0)
        def _():
            within(k + 2, st1)
            within(k, st2)

            @pl.when(k == 5)
            def _():
                first()

        @pl.when(lax.rem(i, 2) == 1)
        def _():
            within(k - 1, send_q)
            within(k - 1, st3)

            @pl.when(k == 1)
            def _():
                e_second()

            @pl.when(k == 2)
            def _():
                e_third()

            within(k - 2, st4)
            within(k - 3, st5)

        now = i == computed[0]
        j = jnp.int32(0)
        for at in computed[1:]:
            now = jnp.logical_or(now, i == at)
            j = j + jnp.where(i >= at, 1, 0)

        @pl.when(now)
        def _():
            compute(j)

        return carry

    lax.fori_loop(0, 2 * (chunks + 3), half_slot, 0)

    low[...] = (adapter_scale * lowg[...]).astype(BF16)

    def core_copy():
        return remote(A.at[:, 1 - c], A_core, r_send.at[0], r_recv.at[0], CM)

    def reduce_copy(o):
        return remote(A_sum.at[chip(o)], A_recv.at[o], r_send.at[o], r_recv.at[o], chip_device(o))

    def spread_copy(o, index):
        return remote(A_all.at[index, c], A_all.at[index, c], a_send.at[o], a_recv.at[o], chip_device(o))

    def return_copy(c_):
        return remote(A_all.at[:, c_], A_all.at[:, c_], a_send.at[0], a_recv.at[0], CM)

    def adapter_pieces():
        both = (adapter_scale * lowg[...]).T.astype(BF16)

        def down_grad(m, carry):
            for c_ in range(2):
                cols = pl.ds(pl.multiple_of((2 * m + c_) * BLOCK, BLOCK), BLOCK)
                A[m, c_, :, 0:256] = dot(both, E[:, :, cols].reshape(2 * BLOCK, BLOCK)).astype(BF16)
            return carry

        lax.fori_loop(0, 8, down_grad, 0, unroll=2)
        core_copy().start()

    def adapter_chip():
        core_copy().wait_recv()
        A_sum[...] = (A[:, c].astype(F32) + A_core[...].astype(F32)).astype(BF16)
        for o in range(1, 8):
            reduce_copy(o).start()

    def adapter_sums():
        sum_ = A_sum[me].astype(F32)
        for o in range(1, 8):
            reduce_copy(o).wait_recv()
            sum_ = sum_ + A_recv[o].astype(F32)
        A_all[me, c] = sum_
        for o in range(1, 8):
            spread_copy(o, me).start()

    def back_place(i):
        far = jnp.logical_or(i == 2, i == 3)
        dx = jnp.where(far, 2, jnp.where(i < 6, 1 + 2 * lax.rem(i, 2), 0))
        other = jnp.where(far, 3 - i, jnp.where(i < 6, 1 - i // 4, 7 - i))
        return dx, other

    def z_first_copy(a):
        s = z_coords[a][0]
        i = 3 if a == 0 else 2
        return remote(stage.at[i, s], z_first.at[a], zf_send.at[a], zf_recv.at[a], z_peer(a))

    def x_part_copy(d, e, s):
        i = (4 if e == 0 else 0) + d
        return remote(stage.at[i, s], x_part.at[d, e, s], xp_send.at[d, e, s], xp_recv.at[d, e, s], x_peer(1 if d == 0 else 3))

    def z_part_copy(a):
        return remote(z_sum.at[a], z_part.at[a], zp_send.at[a], zp_recv.at[a], z_peer(a))

    def far_copy():
        return remote(z_first_sum, x_far, far_send.at[0], far_recv.at[0], x_peer(2))

    def back(i, carry):
        @pl.when(i == 2)
        def _():
            adapter_pieces()

        @pl.when(i == 4)
        def _():
            adapter_chip()

        @pl.when(i == 7)
        def _():
            adapter_sums()

        dx, other = back_place(i)
        p = lax.rem(x + dx, 4) * 2 + jnp.where(other == 1, 1 - zh, zh)
        for b in range(2):
            r = 2 * p + b
            r_y, r_z, r_c = r // 4, lax.rem(r // 2, 2), lax.rem(r, 2)
            wide = jnp.concatenate([W[j, r_y, r_z, r_c] for j in range(chunks)], axis=1)
            acc = dot_nt(dkv[...], wide)
            acc = acc + dot(low[...], down[:, pl.ds(pl.multiple_of(r * BLOCK, BLOCK), BLOCK)])
            stage[i, :, :, b * BLOCK : (b + 1) * BLOCK] = acc.astype(BF16).reshape(2, BLOCK, BLOCK)

        @pl.when(i == 2)
        def _():
            z_first_copy(2).start()
            z_first_copy(1).start()

        @pl.when(i == 3)
        def _():
            z_first_copy(0).start()

        for d in range(2):
            for e in range(2):

                @pl.when(i == (4 if e == 0 else 0) + d)
                def _(d=d, e=e):
                    x_part_copy(d, e, 1 - zl).start()
                    x_part_copy(d, e, zl).start()

        return carry

    lax.fori_loop(0, 8, back, 0)

    total = stage[3, zl].astype(F32)
    for a in range(3):
        z_first_copy(a).wait_recv()
        total = total + z_first[a].astype(F32)
    z_first_sum[...] = total.astype(BF16)
    far_copy().start()

    def drain(j, carry):
        for n in range(14):
            w_out(j, n).wait_send()
        for t in range(2):
            q_out(j, t).wait_send()
        return carry

    lax.fori_loop(0, chunks, drain, 0)
    for a in range(3):
        ez_out(a).wait_send()
    for d in range(2):
        for k in range(4):
            ex_out(d, k).wait_send()
        for m in range(2):
            ef_out(d, m).wait_send()
    len_copy(zl).wait_send()

    def over_x(e, s):
        sum_ = stage[7 - e, s].astype(F32)
        for d in range(2):
            x_part_copy(d, e, s).wait_recv()
            sum_ = sum_ + x_part[d, e, s].astype(F32)
        return sum_

    for a in (2, 1, 0):
        z_sum[a] = over_x(0 if a == 0 else 1, z_coords[a][0]).astype(BF16)
        z_part_copy(a).start()

    for o in range(1, 8):
        spread_copy(o, chip(8 - o)).wait_recv()
    return_copy(c).start()

    return_copy(1 - c).wait_recv()
    for r in range(16):
        first_up = r // 2 % 2 * half + (r // 4 * 2 + r % 2) * FEATURES
        kd_ref[:, r * 256 : r * 256 + 256] = A_all[r // 2, r % 2, 0:16, 0:256]
        vd_ref[:, r * 256 : r * 256 + 256] = A_all[r // 2, r % 2, 16:32, 0:256]
        ku_ref[:, pl.ds(first_up, FEATURES)] = A_all[r // 2, r % 2, 0:16, 256:384]
        vu_ref[:, pl.ds(first_up, FEATURES)] = A_all[r // 2, r % 2, 16:32, 256:384]

    total = over_x(0, zl)
    far_copy().wait_recv()
    total = total + x_far[...].astype(F32)
    for a in (2, 1, 0):
        z_part_copy(a).wait_recv()
        total = total + z_part[a].astype(F32)
    out_ref[...] = total.astype(BF16)

    for a in range(3):
        z_first_copy(a).wait_send()
        z_part_copy(a).wait_send()
    for d in range(2):
        for e in range(2):
            for s in range(2):
                x_part_copy(d, e, s).wait_send()
    far_copy().wait_send()
    core_copy().wait_send()
    for o in range(1, 8):
        reduce_copy(o).wait_send()
        spread_copy(o, me).wait_send()
    return_copy(c).wait_send()


def settle(*refs):
    sem = refs[-1]
    copies = [pltpu.make_async_copy(refs[i], refs[5 + i], sem.at[i]) for i in range(5)]
    for copy in copies:
        copy.start()
    for copy in copies:
        copy.wait()


def per_device(
    enc_states, queries, cotangent, enc_lengths, key_weight, value_weight, key_down, key_up, value_down, value_up
):
    inner = queries.shape[2]
    chunks = inner // 2 // FEATURES
    width = key_down.shape[1]
    columns = enc_states.shape[1]
    rows = queries.shape[1]
    hbm = pl.BlockSpec(memory_space=pl.ANY)
    vmem = pl.BlockSpec(memory_space=pltpu.VMEM)
    dma = pltpu.SemaphoreType.DMA
    piece = (BLOCK, columns)
    results = pl.pallas_call(
        functools.partial(kernel, chunks),
        out_shape=(
            jax.ShapeDtypeStruct((BLOCK, columns), BF16),
            jax.ShapeDtypeStruct((16, width), F32),
            jax.ShapeDtypeStruct((16, inner), F32),
            jax.ShapeDtypeStruct((16, width), F32),
            jax.ShapeDtypeStruct((16, inner), F32),
        ),
        in_specs=[hbm, hbm, hbm, pl.BlockSpec(memory_space=pltpu.SMEM)] + [hbm] * 6,
        out_specs=(vmem,) * 5,
        scratch_shapes=[
            pltpu.VMEM((chunks, 4, 2, 2, BLOCK, PACK), BF16),
            pltpu.VMEM((2, BLOCK, width), BF16),
            pltpu.VMEM((chunks, 2, rows, PACK), BF16),
            pltpu.VMEM((2, 8, 128), jnp.int32),
            pltpu.VMEM((32, width), BF16),
            pltpu.VMEM((2, 16, inner // 2), BF16),
            pltpu.VMEM((chunks, 32, PACK), BF16),
            pltpu.VMEM((2 * BLOCK, 32), BF16),
            pltpu.VMEM((32, 2 * BLOCK), BF16),
            pltpu.VMEM((2 * BLOCK, 32), F32),
            pltpu.VMEM((2 * BLOCK, chunks * PACK), BF16),
            pltpu.VMEM((8, 2) + piece, BF16),
            pltpu.VMEM((2, 2, 2) + piece, BF16),
            pltpu.VMEM((3,) + piece, BF16),
            pltpu.VMEM(piece, BF16),
            pltpu.VMEM((3,) + piece, BF16),
            pltpu.VMEM((3,) + piece, BF16),
            pltpu.VMEM(piece, BF16),
            pltpu.VMEM((8, 2, 32, 384), BF16),
            pltpu.VMEM((8, 32, 384), BF16),
            pltpu.VMEM((8, 32, 384), BF16),
            pltpu.VMEM((8, 32, 384), BF16),
            pltpu.VMEM((8, 2, 32, 384), F32),
            dma((5,)),
            dma((chunks, 2)),
            dma((chunks, 2)),
            dma((chunks, 14)),
            dma((chunks, 14)),
            dma((chunks, 2)),
            dma((chunks, 2)),
            dma((3,)),
            dma((3,)),
            dma((2, 4)),
            dma((2, 4)),
            dma((2, 2)),
            dma((2, 2)),
            dma((1,)),
            dma((1,)),
            dma((3,)),
            dma((3,)),
            dma((2, 2, 2)),
            dma((2, 2, 2)),
            dma((3,)),
            dma((3,)),
            dma((1,)),
            dma((1,)),
            dma((8,)),
            dma((8,)),
            dma((8,)),
            dma((8,)),
        ],
        compiler_params=pltpu.CompilerParams(
            collective_id=0, has_side_effects=True, vmem_limit_bytes=60 * 1024 * 1024
        ),
        name="adapter_backward",
    )(
        enc_states, queries, cotangent, enc_lengths, key_weight, value_weight,
        key_down[0].T, key_up, value_down[0].T, value_up,
    )
    out, kd_grad, ku_grad, vd_grad, vu_grad = pl.pallas_call(
        settle,
        out_shape=tuple(jax.ShapeDtypeStruct(r.shape, r.dtype) for r in results),
        in_specs=[vmem] * 5,
        out_specs=(hbm,) * 5,
        scratch_shapes=[dma((5,))],
        name="results",
    )(*results)
    return out, kd_grad.T[None], ku_grad[None], vd_grad.T[None], vu_grad[None]


def solution(mesh):
    return jax.shard_map(
        per_device,
        mesh=mesh,
        in_specs=(
            P("dp", "section"),
            P("section", "dp", None),
            P("section", "dp", None),
            P("dp"),
            P("section", "dp", None),
            P("section", "dp", None),
            P("section", None, None),
            P("section", None, None),
            P("section", None, None),
            P("section", None, None),
        ),
        out_specs=(
            P("dp", "section"),
            P("section", None, None),
            P("section", None, None),
            P("section", None, None),
            P("section", None, None),
        ),
        check_vma=False,
    )
```

```python
import functools

import jax
import jax.numpy as jnp
from jax import lax
from jax.experimental import pallas as pl
from jax.experimental.pallas import tpu as pltpu
from jax.sharding import PartitionSpec as P

HEAD_DIM = 64
MESH = pl.DeviceIdType.MESH
adapter_scale = 0.5
masked_score = -1e30
F32 = jnp.float32
BF16 = jnp.bfloat16

FEATURES = 128
PACK = 2 * FEATURES
BLOCK = 256

NT = (((1,), (1,)), ((), ()))


def dot(a, b):
    return jnp.dot(a, b, preferred_element_type=F32)


def dot_nt(a, b):
    return lax.dot_general(a, b, NT, preferred_element_type=F32)


def kernel(
    chunks,
    enc_hbm, q_hbm, g_hbm, len_ref, kw_hbm, vw_hbm, kd_hbm, ku_hbm, vd_hbm, vu_hbm,
    out_ref, kd_ref, ku_ref, vd_ref, vu_ref,
    W, E, QG, lens, down, up, up_pack, low, low_t, lowg, dkv,
    stage, x_part, z_first, z_first_sum, z_sum, z_part, x_far,
    A, A_core, A_sum, A_recv, A_all, down_out, up_out,
    local_sem, out_sem, own_sem, q_own_sem, w_send, w_recv, q_send, q_recv,
    ez_send, ez_recv, ex_send, ex_recv, ef_send, ef_recv, len_send, len_recv,
    zf_send, zf_recv, xp_send, xp_recv, zp_send, zp_recv, far_send, far_recv,
    r_send, r_recv, a_send, a_recv,
):
    dp = lax.axis_index("dp")
    sec = lax.axis_index("section")
    c, zl, y = lax.rem(dp, 2), lax.rem(dp // 2, 2), dp // 4
    x, zh = sec // 2, lax.rem(sec, 2)
    yp, ym, yo = lax.rem(y + 1, 4), lax.rem(y + 3, 4), lax.rem(y + 2, 4)
    half = chunks * FEATURES
    columns = enc_hbm.shape[1]

    def did(y_, z_, c_):
        return ((y_ * 2 + z_) * 2 + c_, sec)

    UP, DN, ZM, CM = did(yp, zl, c), did(ym, zl, c), did(y, 1 - zl, c), did(y, zl, 1 - c)

    me = dp // 2

    def chip(o):
        return lax.rem(me + o, 8)

    def chip_device(o):
        return (chip(o) * 2 + c, sec)

    def sec_of(dx, zh_):
        return lax.rem(x + dx, 4) * 2 + zh_

    def x_peer(dx):
        return (dp, sec_of(dx, zh))

    z_coords = ((1 - zl, zh), (zl, 1 - zh), (1 - zl, 1 - zh))

    def z_peer(a):
        z_, h_ = z_coords[a]
        return ((y * 2 + z_) * 2 + c, x * 2 + h_)

    def remote(src, dst, send, recv, dev):
        return pltpu.make_async_remote_copy(
            src_ref=src, dst_ref=dst, send_sem=send, recv_sem=recv, device_id=dev, device_id_type=MESH
        )

    barrier = pltpu.get_barrier_semaphore()
    for o in range(1, 8):
        pl.semaphore_signal(barrier, inc=1, device_id=chip_device(o), device_id_type=MESH)
    for dev in (CM, x_peer(1), x_peer(2), x_peer(3), z_peer(1), z_peer(2)):
        pl.semaphore_signal(barrier, inc=1, device_id=dev, device_id_type=MESH)

    def section_columns(p):
        return pl.ds(pl.multiple_of(p * columns, columns), columns)

    def features(side, j):
        return pl.ds(pl.multiple_of(side * half + j * FEATURES, FEATURES), FEATURES)

    def lanes(t):
        return pl.ds(t * FEATURES, FEATURES)

    def own_copy(j, t):
        w = (kw_hbm, vw_hbm)[t]
        return pltpu.make_async_copy(w.at[0, :, features(zl, j)], W.at[j, y, zl, c, :, lanes(t)], own_sem.at[j, t])

    def q_own(j, t):
        q = (q_hbm, g_hbm)[t]
        return pltpu.make_async_copy(q.at[0, :, features(zl, j)], QG.at[j, zl, :, lanes(t)], q_own_sem.at[j, t])

    up_columns = pl.ds(pl.multiple_of(zl * half, half), half)
    local = [
        pltpu.make_async_copy(enc_hbm, E.at[zl, :, section_columns(sec)], local_sem.at[0]),
        pltpu.make_async_copy(kd_hbm, down.at[0:16], local_sem.at[1]),
        pltpu.make_async_copy(vd_hbm, down.at[16:32], local_sem.at[2]),
        pltpu.make_async_copy(ku_hbm.at[0, :, up_columns], up.at[0], local_sem.at[3]),
        pltpu.make_async_copy(vu_hbm.at[0, :, up_columns], up.at[1], local_sem.at[4]),
    ]
    lens[zl] = jnp.full(lens.shape[1:], len_ref[0], jnp.int32)
    pl.semaphore_wait(barrier, 13)

    def pair(j, y_, c_):
        return W.at[j, y_, :, c_]

    def w_copy(j, n, dev, ref):
        return remote(ref, ref, w_send.at[j, n], w_recv.at[j, n], dev)

    def w_out(j, n):
        if n in (0, 9):
            t = 0 if n == 0 else 1
            w = (kw_hbm, vw_hbm)[t]
            return remote(
                w.at[0, :, features(1 - zl, j)], W.at[j, y, zl, c, :, lanes(t)], w_send.at[j, n], w_recv.at[j, n], ZM
            )
        if n in (1, 2, 10, 11):
            t = 0 if n in (1, 2) else 1
            w = (kw_hbm, vw_hbm)[t]
            return remote(
                w.at[0, :, features(zl, j)], W.at[j, y, zl, c, :, lanes(t)], w_send.at[j, n], w_recv.at[j, n],
                UP if n in (1, 10) else DN,
            )
        if n in (12, 13):
            return w_copy(j, n, UP if n == 12 else DN, W.at[j, y, 1 - zl, c])
        if n == 3:
            return w_copy(j, n, UP, W.at[j, ym, 0, c])
        if n == 4:
            return w_copy(j, n, DN, W.at[j, yp, 1, c])
        return w_copy(j, n, CM, pair(j, (y, ym, yp, yo)[n - 5], c))

    def w_in(j, n):
        if n in (0, 9):
            return w_copy(j, n, ZM, W.at[j, y, 1 - zl, c, :, lanes(0 if n == 0 else 1)])
        if n in (1, 2, 10, 11):
            up_ = n in (1, 10)
            t = 0 if n in (1, 2) else 1
            return w_copy(j, n, DN if up_ else UP, W.at[j, ym if up_ else yp, zl, c, :, lanes(t)])
        if n in (12, 13):
            return w_copy(j, n, DN if n == 12 else UP, W.at[j, ym if n == 12 else yp, 1 - zl, c])
        if n in (3, 4):
            return w_copy(j, n, DN if n == 3 else UP, W.at[j, yo, n - 3, c])
        return w_copy(j, n, CM, pair(j, (y, ym, yp, yo)[n - 5], 1 - c))

    def go(j, *ns):
        for n in ns:
            w_out(j, n).start()

    def wt(j, *ns):
        for n in ns:
            w_in(j, n).wait_recv()

    def st1(j):
        go(j, 0, 9, 1, 2, 10, 11)

    def st2(j):
        for t in range(2):
            own_copy(j, t).wait()
        wt(j, 0, 9)
        go(j, 12, 13, 5)

    def st3(j):
        wt(j, 1, 2, 10, 11, 12, 13)
        go(j, 3, 4, 6, 7)

    def st4(j):
        wt(j, 3, 4)
        go(j, 8)

    def st5(j):
        wt(j, 5, 6, 7, 8)

    def q_out(j, t):
        q = (q_hbm, g_hbm)[t]
        return remote(
            q.at[0, :, features(1 - zl, j)], QG.at[j, zl, :, lanes(t)], q_send.at[j, t], q_recv.at[j, t], ZM
        )

    def q_in(j, t):
        ref = QG.at[j, 1 - zl, :, lanes(t)]
        return remote(ref, ref, q_send.at[j, t], q_recv.at[j, t], ZM)

    def send_q(j):
        for t in range(2):
            q_out(j, t).start()

    def e_piece(s, p):
        return E.at[s, :, section_columns(p)]

    def ez_out(a):
        return remote(enc_hbm, e_piece(zl, sec), ez_send.at[a], ez_recv.at[a], z_peer(a))

    def ez_in(a):
        z_, h_ = z_coords[a]
        ref = e_piece(z_, x * 2 + h_)
        return remote(ref, ref, ez_send.at[a], ez_recv.at[a], z_peer(a))

    def ex_out(d, k):
        dev = x_peer(1 if d == 0 else 3)
        if k == 0:
            return remote(enc_hbm, e_piece(zl, sec), ex_send.at[d, k], ex_recv.at[d, k], dev)
        z_, h_ = z_coords[k - 1]
        ref = e_piece(z_, x * 2 + h_)
        return remote(ref, ref, ex_send.at[d, k], ex_recv.at[d, k], dev)

    def ex_in(d, m, s):
        k = 2 * m + jnp.where(s == zl, 0, 1)
        ref = e_piece(s, sec_of(3 if d == 0 else 1, 1 - zh if m else zh))
        return remote(ref, ref, ex_send.at[d, k], ex_recv.at[d, k], x_peer(3 if d == 0 else 1))

    def ef_out(d, m):
        ref = e_piece(d, sec_of(3 if d == 0 else 1, 1 - zh if m else zh))
        return remote(ref, ref, ef_send.at[d, m], ef_recv.at[d, m], x_peer(1 if d == 0 else 3))

    def ef_in(d, m):
        ref = e_piece(d, sec_of(2, 1 - zh if m else zh))
        return remote(ref, ref, ef_send.at[d, m], ef_recv.at[d, m], x_peer(3 if d == 0 else 1))

    def e_second(a):
        ez_in(a).wait_recv()
        for d in range(2):
            ex_out(d, a + 1).start()

    def e_third(m):
        for d in range(2):
            ex_in(d, m, d).wait_recv()
            ef_out(d, m).start()

    def len_copy(s):
        return remote(lens.at[s], lens.at[s], len_send.at[0], len_recv.at[0], ZM)

    st1(0)
    st1(1)
    for a in range(3):
        ez_out(a).start()
    for d in range(2):
        ex_out(d, 0).start()
    len_copy(zl).start()

    for j in range(chunks):
        for t in range(2):
            own_copy(j, t).start()
    for copy in local:
        copy.start()
    for j in range(chunks):
        for t in range(2):
            q_own(j, t).start()
    A[...] = jnp.zeros(A.shape, BF16)

    def first():
        for copy in local:
            copy.wait()
        len_copy(1 - zl).wait_recv()
        for m in range(2):
            for d in range(2):
                ex_in(d, m, 1 - d).wait_recv()
                ef_in(d, m).wait_recv()
        states = E[...].reshape(2 * BLOCK, E.shape[2])
        both = dot_nt(states, down[...])
        low[...] = both.astype(BF16)
        low_t[...] = both.T.astype(BF16)
        lowg[...] = jnp.zeros(lowg.shape, F32)
        up_pack[...] = jnp.zeros(up_pack.shape, BF16)
        for j in range(chunks):
            for t in range(2):
                up_pack[j, 16 * t : 16 * t + 16, FEATURES * t : FEATURES * t + FEATURES] = up[
                    t, :, FEATURES * j : FEATURES * j + FEATURES
                ]

    def compute(j):
        for t in range(2):
            q_own(j, t).wait()
            q_in(j, t).wait_recv()
        weight = W[j].reshape(16 * BLOCK, PACK)
        base = dot(E[...].reshape(2 * BLOCK, E.shape[2]), weight)
        base = base + adapter_scale * dot(low[...], up_pack[j])
        here_columns = pl.ds(pl.multiple_of(j * PACK, PACK), PACK)
        dkv[:, here_columns] = base.astype(BF16)
        lane = lax.broadcasted_iota(jnp.int32, (1, FEATURES), 1) // HEAD_DIM
        index = lax.broadcasted_iota(jnp.int32, (BLOCK, 1), 0)
        zero = jnp.zeros((), BF16)

        def sequence(s, carry):
            here_rows = pl.ds(pl.multiple_of(s * BLOCK, BLOCK), BLOCK)
            rows = dkv[here_rows, here_columns]
            key_rows, value_rows = rows[:, :FEATURES], rows[:, FEATURES:]
            q, g = QG[j, s, :, :FEATURES], QG[j, s, :, FEATURES:]
            visible = index < lens[s, 0:1, 0:1]
            scores = dot_nt(jnp.concatenate([jnp.where(lane == h, key_rows, zero) for h in range(2)], axis=0), q)
            dprobs = dot_nt(jnp.concatenate([jnp.where(lane == h, value_rows, zero) for h in range(2)], axis=0), g)
            all_probs, all_dscores = [], []
            for h in range(2):
                masked = jnp.where(visible, scores[BLOCK * h : BLOCK * h + BLOCK], masked_score)
                expo = jnp.exp(masked - jnp.max(masked, axis=0, keepdims=True))
                probs = (expo * (1.0 / jnp.sum(expo, axis=0, keepdims=True))).astype(BF16)
                wide = probs.astype(F32)
                dprob = dprobs[BLOCK * h : BLOCK * h + BLOCK]
                inner = jnp.sum(wide * dprob, axis=0, keepdims=True)
                all_probs.append(probs)
                all_dscores.append((wide * (dprob - inner)).astype(BF16))
            dvalues = dot(jnp.concatenate(all_probs, axis=0), g)
            dkeys = dot(jnp.concatenate(all_dscores, axis=0), q)
            both = [jnp.where(lane == 0, d[:BLOCK], d[BLOCK:]) for d in (dkeys, dvalues)]
            dkv[here_rows, here_columns] = jnp.concatenate(both, axis=1).astype(BF16)
            return carry

        lax.fori_loop(0, 2, sequence, 0)
        grad = dkv[:, here_columns]
        lowg[...] += dot_nt(grad, up_pack[j])
        up_grad = adapter_scale * dot(low_t[...], grad)
        r = (j // 2) * 2 + zl
        r_core = lax.rem(j, 2)
        for t in range(2):
            A[r, r_core, pl.ds(16 * t, 16), 256:384] = up_grad[
                16 * t : 16 * t + 16, FEATURES * t : FEATURES * t + FEATURES
            ].astype(BF16)

    def within(j, fn):
        @pl.when(jnp.logical_and(j >= 0, j < chunks))
        def _():
            fn(j)

    computed = (10, 12, 13, 14, 15, 17, 19, 21)

    def half_slot(i, carry):
        k = i // 2

        @pl.when(lax.rem(i, 2) == 0)
        def _():
            within(k + 2, st1)
            within(k, st2)

        @pl.when(lax.rem(i, 2) == 1)
        def _():
            within(k - 1, send_q)
            within(k - 1, st3)

            within(k - 2, st4)
            within(k - 3, st5)

        @pl.when(i == 2)
        def _():
            e_second(2)
            e_second(0)

        @pl.when(i == 4)
        def _():
            e_second(1)

        @pl.when(i == 6)
        def _():
            e_third(0)

        @pl.when(i == 7)
        def _():
            e_third(1)

        @pl.when(i == 10)
        def _():
            first()

        now = i == computed[0]
        j = jnp.int32(0)
        for at in computed[1:]:
            now = jnp.logical_or(now, i == at)
            j = j + jnp.where(i >= at, 1, 0)

        @pl.when(now)
        def _():
            compute(j)

        return carry

    lax.fori_loop(0, 2 * (chunks + 3), half_slot, 0)

    low[...] = (adapter_scale * lowg[...]).astype(BF16)

    def core_copy():
        return remote(A.at[:, 1 - c], A_core, r_send.at[0], r_recv.at[0], CM)

    def reduce_copy(o):
        return remote(A_sum.at[chip(o)], A_recv.at[o], r_send.at[o], r_recv.at[o], chip_device(o))

    def spread_copy(o, index):
        return remote(A_all.at[index, c], A_all.at[index, c], a_send.at[o], a_recv.at[o], chip_device(o))

    def return_copy(c_):
        return remote(A_all.at[:, c_], A_all.at[:, c_], a_send.at[0], a_recv.at[0], CM)

    def adapter_pieces():
        both = (adapter_scale * lowg[...]).T.astype(BF16)

        def down_grad(m, carry):
            for c_ in range(2):
                cols = pl.ds(pl.multiple_of((2 * m + c_) * BLOCK, BLOCK), BLOCK)
                A[m, c_, :, 0:256] = dot(both, E[:, :, cols].reshape(2 * BLOCK, BLOCK)).astype(BF16)
            return carry

        lax.fori_loop(0, 8, down_grad, 0, unroll=2)
        core_copy().start()

    def adapter_chip():
        core_copy().wait_recv()
        A_sum[...] = (A[:, c].astype(F32) + A_core[...].astype(F32)).astype(BF16)
        for o in range(1, 8):
            reduce_copy(o).start()

    def adapter_sums():
        sum_ = A_sum[me].astype(F32)
        for o in range(1, 8):
            reduce_copy(o).wait_recv()
            sum_ = sum_ + A_recv[o].astype(F32)
        A_all[me, c] = sum_.astype(BF16)
        for o in range(1, 8):
            spread_copy(o, me).start()

    def back_place(i):
        far = jnp.logical_or(i == 2, i == 3)
        dx = jnp.where(far, 2, jnp.where(i < 6, 1 + 2 * lax.rem(i, 2), 0))
        other = jnp.where(far, 3 - i, jnp.where(i < 6, 1 - i // 4, 7 - i))
        return dx, other

    def z_first_copy(a):
        s = z_coords[a][0]
        i = 3 if a == 0 else 2
        return remote(stage.at[i, s], z_first.at[a], zf_send.at[a], zf_recv.at[a], z_peer(a))

    def x_part_copy(d, e, s):
        i = (4 if e == 0 else 0) + d
        return remote(stage.at[i, s], x_part.at[d, e, s], xp_send.at[d, e, s], xp_recv.at[d, e, s], x_peer(1 if d == 0 else 3))

    def z_part_copy(a):
        return remote(z_sum.at[a], z_part.at[a], zp_send.at[a], zp_recv.at[a], z_peer(a))

    def far_copy():
        return remote(z_first_sum, x_far, far_send.at[0], far_recv.at[0], x_peer(2))

    def back(i, carry):
        @pl.when(i == 4)
        def _():
            adapter_pieces()

        @pl.when(i == 6)
        def _():
            adapter_chip()

        dx, other = back_place(i)
        p = lax.rem(x + dx, 4) * 2 + jnp.where(other == 1, 1 - zh, zh)
        for b in range(2):
            r = 2 * p + b
            r_y, r_z, r_c = r // 4, lax.rem(r // 2, 2), lax.rem(r, 2)
            wide = jnp.concatenate([W[j, r_y, r_z, r_c] for j in range(chunks)], axis=1)
            acc = dot_nt(dkv[...], wide)
            acc = acc + dot(low[...], down[:, pl.ds(pl.multiple_of(r * BLOCK, BLOCK), BLOCK)])
            stage[i, :, :, b * BLOCK : (b + 1) * BLOCK] = acc.astype(BF16).reshape(2, BLOCK, BLOCK)

        @pl.when(i == 2)
        def _():
            z_first_copy(2).start()
            z_first_copy(1).start()

        @pl.when(i == 3)
        def _():
            z_first_copy(0).start()

        for d in range(2):
            for e in range(2):

                @pl.when(i == (4 if e == 0 else 0) + d)
                def _(d=d, e=e):
                    x_part_copy(d, e, 1 - zl).start()
                    x_part_copy(d, e, zl).start()

        return carry

    lax.fori_loop(0, 8, back, 0)

    def over_x(e, s):
        sum_ = stage[7 - e, s].astype(F32)
        for d in range(2):
            x_part_copy(d, e, s).wait_recv()
            sum_ = sum_ + x_part[d, e, s].astype(F32)
        return sum_

    def over_x_to(a):
        z_sum[a] = over_x(0 if a == 0 else 1, z_coords[a][0]).astype(BF16)
        z_part_copy(a).start()

    over_x_to(2)
    over_x_to(1)
    total = stage[3, zl].astype(F32)
    for a in range(3):
        z_first_copy(a).wait_recv()
        total = total + z_first[a].astype(F32)
    z_first_sum[...] = total.astype(BF16)
    far_copy().start()

    adapter_sums()
    over_x_to(0)

    def drain(j, carry):
        for n in range(14):
            w_out(j, n).wait_send()
        for t in range(2):
            q_out(j, t).wait_send()
        return carry

    lax.fori_loop(0, chunks, drain, 0)
    for a in range(3):
        ez_out(a).wait_send()
    for d in range(2):
        for k in range(4):
            ex_out(d, k).wait_send()
        for m in range(2):
            ef_out(d, m).wait_send()
    len_copy(zl).wait_send()

    for o in range(1, 8):
        spread_copy(o, chip(8 - o)).wait_recv()
    return_copy(c).start()

    return_copy(1 - c).wait_recv()
    for r in range(16):
        first_up = r // 2 % 2 * half + (r // 4 * 2 + r % 2) * FEATURES
        for t in range(2):
            rows = slice(16 * t, 16 * t + 16)
            down_out[t, :, r * 256 : r * 256 + 256] = A_all[r // 2, r % 2, rows, 0:256].astype(F32)
            up_out[t, :, pl.ds(first_up, FEATURES)] = A_all[r // 2, r % 2, rows, 256:384].astype(F32)
    leave = [
        pltpu.make_async_copy(source.at[t], ref, out_sem.at[n])
        for n, (source, t, ref) in enumerate(
            ((down_out, 0, kd_ref), (up_out, 0, ku_ref), (down_out, 1, vd_ref), (up_out, 1, vu_ref))
        )
    ]
    for copy in leave:
        copy.start()

    total = over_x(0, zl)
    for a in (2, 1, 0):
        z_part_copy(a).wait_recv()
        total = total + z_part[a].astype(F32)
    far_copy().wait_recv()
    out_ref[...] = (total + x_far[...].astype(F32)).astype(BF16)

    for copy in leave:
        copy.wait()
    for a in range(3):
        z_first_copy(a).wait_send()
        z_part_copy(a).wait_send()
    for d in range(2):
        for e in range(2):
            for s in range(2):
                x_part_copy(d, e, s).wait_send()
    far_copy().wait_send()
    core_copy().wait_send()
    for o in range(1, 8):
        reduce_copy(o).wait_send()
        spread_copy(o, me).wait_send()
    return_copy(c).wait_send()


def settle(*refs):
    sources, targets, held, sem = refs[:5], refs[5:10], refs[10:15], refs[15]
    into = [pltpu.make_async_copy(sources[i], held[i], sem.at[0, i]) for i in range(5)]
    out = [pltpu.make_async_copy(held[i], targets[i], sem.at[1, i]) for i in range(5)]
    for copy in into:
        copy.start()
    for i in range(5):
        into[i].wait()
        out[i].start()
    for copy in out:
        copy.wait()


def per_device(
    enc_states, queries, cotangent, enc_lengths, key_weight, value_weight, key_down, key_up, value_down, value_up
):
    inner = queries.shape[2]
    chunks = inner // 2 // FEATURES
    width = key_down.shape[1]
    columns = enc_states.shape[1]
    rows = queries.shape[1]
    hbm = pl.BlockSpec(memory_space=pl.ANY)
    vmem = pl.BlockSpec(memory_space=pltpu.VMEM)
    dma = pltpu.SemaphoreType.DMA
    piece = (BLOCK, columns)
    results = pl.pallas_call(
        functools.partial(kernel, chunks),
        out_shape=(
            jax.ShapeDtypeStruct((BLOCK, columns), BF16),
            jax.ShapeDtypeStruct((16, width), F32),
            jax.ShapeDtypeStruct((16, inner), F32),
            jax.ShapeDtypeStruct((16, width), F32),
            jax.ShapeDtypeStruct((16, inner), F32),
        ),
        in_specs=[hbm, hbm, hbm, pl.BlockSpec(memory_space=pltpu.SMEM)] + [hbm] * 6,
        out_specs=(vmem,) + (hbm,) * 4,
        scratch_shapes=[
            pltpu.VMEM((chunks, 4, 2, 2, BLOCK, PACK), BF16),
            pltpu.VMEM((2, BLOCK, width), BF16),
            pltpu.VMEM((chunks, 2, rows, PACK), BF16),
            pltpu.VMEM((2, 8, 128), jnp.int32),
            pltpu.VMEM((32, width), BF16),
            pltpu.VMEM((2, 16, inner // 2), BF16),
            pltpu.VMEM((chunks, 32, PACK), BF16),
            pltpu.VMEM((2 * BLOCK, 32), BF16),
            pltpu.VMEM((32, 2 * BLOCK), BF16),
            pltpu.VMEM((2 * BLOCK, 32), F32),
            pltpu.VMEM((2 * BLOCK, chunks * PACK), BF16),
            pltpu.VMEM((8, 2) + piece, BF16),
            pltpu.VMEM((2, 2, 2) + piece, BF16),
            pltpu.VMEM((3,) + piece, BF16),
            pltpu.VMEM(piece, BF16),
            pltpu.VMEM((3,) + piece, BF16),
            pltpu.VMEM((3,) + piece, BF16),
            pltpu.VMEM(piece, BF16),
            pltpu.VMEM((8, 2, 32, 384), BF16),
            pltpu.VMEM((8, 32, 384), BF16),
            pltpu.VMEM((8, 32, 384), BF16),
            pltpu.VMEM((8, 32, 384), BF16),
            pltpu.VMEM((8, 2, 32, 384), BF16),
            pltpu.VMEM((2, 16, width), F32),
            pltpu.VMEM((2, 16, inner), F32),
            dma((5,)),
            dma((4,)),
            dma((chunks, 2)),
            dma((chunks, 2)),
            dma((chunks, 14)),
            dma((chunks, 14)),
            dma((chunks, 2)),
            dma((chunks, 2)),
            dma((3,)),
            dma((3,)),
            dma((2, 4)),
            dma((2, 4)),
            dma((2, 2)),
            dma((2, 2)),
            dma((1,)),
            dma((1,)),
            dma((3,)),
            dma((3,)),
            dma((2, 2, 2)),
            dma((2, 2, 2)),
            dma((3,)),
            dma((3,)),
            dma((1,)),
            dma((1,)),
            dma((8,)),
            dma((8,)),
            dma((8,)),
            dma((8,)),
        ],
        compiler_params=pltpu.CompilerParams(
            collective_id=0, has_side_effects=True, vmem_limit_bytes=60 * 1024 * 1024
        ),
        name="adapter_backward",
    )(
        enc_states, queries, cotangent, enc_lengths, key_weight, value_weight,
        key_down[0].T, key_up, value_down[0].T, value_up,
    )
    out, kd_grad, ku_grad, vd_grad, vu_grad = pl.pallas_call(
        settle,
        out_shape=tuple(jax.ShapeDtypeStruct(r.shape, r.dtype) for r in results),
        in_specs=[hbm] * 5,
        out_specs=(hbm,) * 5,
        scratch_shapes=[pltpu.VMEM(r.shape, r.dtype) for r in results] + [dma((2, 5))],
        name="results",
    )(*results)
    return out, kd_grad.T[None], ku_grad[None], vd_grad.T[None], vu_grad[None]


def solution(mesh):
    return jax.shard_map(
        per_device,
        mesh=mesh,
        in_specs=(
            P("dp", "section"),
            P("section", "dp", None),
            P("section", "dp", None),
            P("dp"),
            P("section", "dp", None),
            P("section", "dp", None),
            P("section", None, None),
            P("section", None, None),
            P("section", None, None),
            P("section", None, None),
        ),
        out_specs=(
            P("dp", "section"),
            P("section", None, None),
            P("section", None, None),
            P("section", None, None),
            P("section", None, None),
        ),
        check_vma=False,
    )
```

```python
import functools

import jax
import jax.numpy as jnp
from jax import lax
from jax.experimental import pallas as pl
from jax.experimental.pallas import tpu as pltpu
from jax.sharding import PartitionSpec as P

HEAD_DIM = 64
MESH = pl.DeviceIdType.MESH
adapter_scale = 0.5
masked_score = -1e30
F32 = jnp.float32
BF16 = jnp.bfloat16

FEATURES = 128
PACK = 2 * FEATURES
BLOCK = 256

NT = (((1,), (1,)), ((), ()))


def dot(a, b):
    return jnp.dot(a, b, preferred_element_type=F32)


def dot_nt(a, b):
    return lax.dot_general(a, b, NT, preferred_element_type=F32)


def kernel(
    chunks,
    enc_hbm, q_hbm, g_hbm, len_ref, kw_hbm, vw_hbm, kd_hbm, ku_hbm, vd_hbm, vu_hbm,
    out_ref, kd_ref, ku_ref, vd_ref, vu_ref,
    W, E, QG, lens, down, up, up_pack, low, low_t, lowg, dkv,
    stage, x_part, z_first, z_first_sum, z_sum, z_part, x_far,
    A, A_core, A_sum, A_recv, A_all, down_out, up_out,
    local_sem, out_sem, own_sem, q_own_sem, w_send, w_recv, q_send, q_recv,
    ez_send, ez_recv, ex_send, ex_recv, ef_send, ef_recv, len_send, len_recv,
    zf_send, zf_recv, xp_send, xp_recv, zp_send, zp_recv, far_send, far_recv,
    r_send, r_recv, a_send, a_recv,
):
    dp = lax.axis_index("dp")
    sec = lax.axis_index("section")
    c, zl, y = lax.rem(dp, 2), lax.rem(dp // 2, 2), dp // 4
    x, zh = sec // 2, lax.rem(sec, 2)
    yp, ym, yo = lax.rem(y + 1, 4), lax.rem(y + 3, 4), lax.rem(y + 2, 4)
    half = chunks * FEATURES
    columns = enc_hbm.shape[1]

    def did(y_, z_, c_):
        return ((y_ * 2 + z_) * 2 + c_, sec)

    UP, DN, ZM, CM = did(yp, zl, c), did(ym, zl, c), did(y, 1 - zl, c), did(y, zl, 1 - c)

    me = dp // 2

    def chip(o):
        return lax.rem(me + o, 8)

    def chip_device(o):
        return (chip(o) * 2 + c, sec)

    def sec_of(dx, zh_):
        return lax.rem(x + dx, 4) * 2 + zh_

    def x_peer(dx):
        return (dp, sec_of(dx, zh))

    z_coords = ((1 - zl, zh), (zl, 1 - zh), (1 - zl, 1 - zh))

    def z_peer(a):
        z_, h_ = z_coords[a]
        return ((y * 2 + z_) * 2 + c, x * 2 + h_)

    def remote(src, dst, send, recv, dev):
        return pltpu.make_async_remote_copy(
            src_ref=src, dst_ref=dst, send_sem=send, recv_sem=recv, device_id=dev, device_id_type=MESH
        )

    barrier = pltpu.get_barrier_semaphore()
    for o in range(1, 8):
        pl.semaphore_signal(barrier, inc=1, device_id=chip_device(o), device_id_type=MESH)
    for dev in (CM, x_peer(1), x_peer(2), x_peer(3), z_peer(1), z_peer(2)):
        pl.semaphore_signal(barrier, inc=1, device_id=dev, device_id_type=MESH)

    def section_columns(p):
        return pl.ds(pl.multiple_of(p * columns, columns), columns)

    def features(side, j):
        return pl.ds(pl.multiple_of(side * half + j * FEATURES, FEATURES), FEATURES)

    def lanes(t):
        return pl.ds(t * FEATURES, FEATURES)

    def own_copy(j, t):
        w = (kw_hbm, vw_hbm)[t]
        return pltpu.make_async_copy(w.at[0, :, features(zl, j)], W.at[j, y, zl, c, :, lanes(t)], own_sem.at[j, t])

    def q_own(j, t):
        q = (q_hbm, g_hbm)[t]
        return pltpu.make_async_copy(q.at[0, :, features(zl, j)], QG.at[j, zl, :, lanes(t)], q_own_sem.at[j, t])

    up_columns = pl.ds(pl.multiple_of(zl * half, half), half)
    local = [
        pltpu.make_async_copy(enc_hbm, E.at[zl, :, section_columns(sec)], local_sem.at[0]),
        pltpu.make_async_copy(kd_hbm, down.at[0:16], local_sem.at[1]),
        pltpu.make_async_copy(vd_hbm, down.at[16:32], local_sem.at[2]),
        pltpu.make_async_copy(ku_hbm.at[0, :, up_columns], up.at[0], local_sem.at[3]),
        pltpu.make_async_copy(vu_hbm.at[0, :, up_columns], up.at[1], local_sem.at[4]),
    ]
    lens[zl] = jnp.full(lens.shape[1:], len_ref[0], jnp.int32)
    pl.semaphore_wait(barrier, 13)

    def pair(j, y_, c_):
        return W.at[j, y_, :, c_]

    def w_copy(j, n, dev, ref):
        return remote(ref, ref, w_send.at[j, n], w_recv.at[j, n], dev)

    def w_out(j, n):
        if n in (0, 9):
            t = 0 if n == 0 else 1
            w = (kw_hbm, vw_hbm)[t]
            return remote(
                w.at[0, :, features(1 - zl, j)], W.at[j, y, zl, c, :, lanes(t)], w_send.at[j, n], w_recv.at[j, n], ZM
            )
        if n in (1, 2, 10, 11):
            t = 0 if n in (1, 2) else 1
            w = (kw_hbm, vw_hbm)[t]
            return remote(
                w.at[0, :, features(zl, j)], W.at[j, y, zl, c, :, lanes(t)], w_send.at[j, n], w_recv.at[j, n],
                UP if n in (1, 10) else DN,
            )
        if n in (12, 13):
            return w_copy(j, n, UP if n == 12 else DN, W.at[j, y, 1 - zl, c])
        if n == 3:
            return w_copy(j, n, UP, W.at[j, ym, 0, c])
        if n == 4:
            return w_copy(j, n, DN, W.at[j, yp, 1, c])
        return w_copy(j, n, CM, pair(j, (y, ym, yp, yo)[n - 5], c))

    def w_in(j, n):
        if n in (0, 9):
            return w_copy(j, n, ZM, W.at[j, y, 1 - zl, c, :, lanes(0 if n == 0 else 1)])
        if n in (1, 2, 10, 11):
            up_ = n in (1, 10)
            t = 0 if n in (1, 2) else 1
            return w_copy(j, n, DN if up_ else UP, W.at[j, ym if up_ else yp, zl, c, :, lanes(t)])
        if n in (12, 13):
            return w_copy(j, n, DN if n == 12 else UP, W.at[j, ym if n == 12 else yp, 1 - zl, c])
        if n in (3, 4):
            return w_copy(j, n, DN if n == 3 else UP, W.at[j, yo, n - 3, c])
        return w_copy(j, n, CM, pair(j, (y, ym, yp, yo)[n - 5], 1 - c))

    def go(j, *ns):
        for n in ns:
            w_out(j, n).start()

    def wt(j, *ns):
        for n in ns:
            w_in(j, n).wait_recv()

    def st1(j):
        go(j, 0, 9, 1, 2, 10, 11)

    def st2(j):
        for t in range(2):
            own_copy(j, t).wait()
        wt(j, 0, 9)
        go(j, 12, 13, 5)

    def st3(j):
        wt(j, 1, 2, 10, 11, 12, 13)
        go(j, 3, 4, 6, 7)

    def st4(j):
        wt(j, 3, 4)
        go(j, 8)

    def st5(j):
        wt(j, 5, 6, 7, 8)

    def q_out(j, t):
        q = (q_hbm, g_hbm)[t]
        return remote(
            q.at[0, :, features(1 - zl, j)], QG.at[j, zl, :, lanes(t)], q_send.at[j, t], q_recv.at[j, t], ZM
        )

    def q_in(j, t):
        ref = QG.at[j, 1 - zl, :, lanes(t)]
        return remote(ref, ref, q_send.at[j, t], q_recv.at[j, t], ZM)

    def send_q(j):
        for t in range(2):
            q_out(j, t).start()

    def e_piece(s, p):
        return E.at[s, :, section_columns(p)]

    def ez_out(a):
        return remote(enc_hbm, e_piece(zl, sec), ez_send.at[a], ez_recv.at[a], z_peer(a))

    def ez_in(a):
        z_, h_ = z_coords[a]
        ref = e_piece(z_, x * 2 + h_)
        return remote(ref, ref, ez_send.at[a], ez_recv.at[a], z_peer(a))

    def ex_out(d, k):
        dev = x_peer(1 if d == 0 else 3)
        if k == 0:
            return remote(enc_hbm, e_piece(zl, sec), ex_send.at[d, k], ex_recv.at[d, k], dev)
        z_, h_ = z_coords[k - 1]
        ref = e_piece(z_, x * 2 + h_)
        return remote(ref, ref, ex_send.at[d, k], ex_recv.at[d, k], dev)

    def ex_in(d, m, s):
        k = 2 * m + jnp.where(s == zl, 0, 1)
        ref = e_piece(s, sec_of(3 if d == 0 else 1, 1 - zh if m else zh))
        return remote(ref, ref, ex_send.at[d, k], ex_recv.at[d, k], x_peer(3 if d == 0 else 1))

    def ef_out(d, m):
        ref = e_piece(d, sec_of(3 if d == 0 else 1, 1 - zh if m else zh))
        return remote(ref, ref, ef_send.at[d, m], ef_recv.at[d, m], x_peer(1 if d == 0 else 3))

    def ef_in(d, m):
        ref = e_piece(d, sec_of(2, 1 - zh if m else zh))
        return remote(ref, ref, ef_send.at[d, m], ef_recv.at[d, m], x_peer(3 if d == 0 else 1))

    def e_second(a):
        ez_in(a).wait_recv()
        for d in range(2):
            ex_out(d, a + 1).start()

    def e_third(m):
        for d in range(2):
            ex_in(d, m, d).wait_recv()
            ef_out(d, m).start()

    def len_copy(s):
        return remote(lens.at[s], lens.at[s], len_send.at[0], len_recv.at[0], ZM)

    st1(0)
    st1(1)
    for a in range(3):
        ez_out(a).start()
    for d in range(2):
        ex_out(d, 0).start()
    len_copy(zl).start()

    for j in range(chunks):
        for t in range(2):
            own_copy(j, t).start()
    for copy in local:
        copy.start()
    for j in range(chunks):
        for t in range(2):
            q_own(j, t).start()
    A[...] = jnp.zeros(A.shape, BF16)

    def first():
        for copy in local:
            copy.wait()
        len_copy(1 - zl).wait_recv()
        for m in range(2):
            for d in range(2):
                ex_in(d, m, 1 - d).wait_recv()
                ef_in(d, m).wait_recv()
        states = E[...].reshape(2 * BLOCK, E.shape[2])
        both = dot_nt(states, down[...])
        low[...] = both.astype(BF16)
        low_t[...] = both.T.astype(BF16)
        up_pack[...] = jnp.zeros(up_pack.shape, BF16)
        for j in range(chunks):
            for t in range(2):
                up_pack[j, 16 * t : 16 * t + 16, FEATURES * t : FEATURES * t + FEATURES] = up[
                    t, :, FEATURES * j : FEATURES * j + FEATURES
                ]

    def compute(j):
        for t in range(2):
            q_own(j, t).wait()
            q_in(j, t).wait_recv()
        weight = W[j].reshape(16 * BLOCK, PACK)
        base = dot(E[...].reshape(2 * BLOCK, E.shape[2]), weight)
        base = base + adapter_scale * dot(low[...], up_pack[j])
        here_columns = pl.ds(pl.multiple_of(j * PACK, PACK), PACK)
        dkv[:, here_columns] = base.astype(BF16)
        lane = lax.broadcasted_iota(jnp.int32, (1, FEATURES), 1) // HEAD_DIM
        index = lax.broadcasted_iota(jnp.int32, (BLOCK, 1), 0)
        zero = jnp.zeros((), BF16)

        def sequence(s, carry):
            here_rows = pl.ds(pl.multiple_of(s * BLOCK, BLOCK), BLOCK)
            rows = dkv[here_rows, here_columns]
            key_rows, value_rows = rows[:, :FEATURES], rows[:, FEATURES:]
            q, g = QG[j, s, :, :FEATURES], QG[j, s, :, FEATURES:]
            visible = index < lens[s, 0:1, 0:1]
            scores = dot_nt(jnp.concatenate([jnp.where(lane == h, key_rows, zero) for h in range(2)], axis=0), q)
            dprobs = dot_nt(jnp.concatenate([jnp.where(lane == h, value_rows, zero) for h in range(2)], axis=0), g)
            all_probs, all_dscores = [], []
            for h in range(2):
                masked = jnp.where(visible, scores[BLOCK * h : BLOCK * h + BLOCK], masked_score)
                expo = jnp.exp(masked - jnp.max(masked, axis=0, keepdims=True))
                probs = (expo * (1.0 / jnp.sum(expo, axis=0, keepdims=True))).astype(BF16)
                wide = probs.astype(F32)
                dprob = dprobs[BLOCK * h : BLOCK * h + BLOCK]
                inner = jnp.sum(wide * dprob, axis=0, keepdims=True)
                all_probs.append(probs)
                all_dscores.append((wide * (dprob - inner)).astype(BF16))
            dvalues = dot(jnp.concatenate(all_probs, axis=0), g)
            dkeys = dot(jnp.concatenate(all_dscores, axis=0), q)
            both = [jnp.where(lane == 0, d[:BLOCK], d[BLOCK:]) for d in (dkeys, dvalues)]
            dkv[here_rows, here_columns] = jnp.concatenate(both, axis=1).astype(BF16)
            return carry

        lax.fori_loop(0, 2, sequence, 0)

    def within(j, fn):
        @pl.when(jnp.logical_and(j >= 0, j < chunks))
        def _():
            fn(j)

    computed = (10, 12, 13, 14, 15, 17, 19, 21)

    def half_slot(i, carry):
        k = i // 2

        @pl.when(lax.rem(i, 2) == 0)
        def _():
            within(k + 2, st1)
            within(k, st2)

        @pl.when(lax.rem(i, 2) == 1)
        def _():
            within(k - 1, send_q)
            within(k - 1, st3)

            within(k - 2, st4)
            within(k - 3, st5)

        @pl.when(i == 2)
        def _():
            e_second(2)
            e_second(0)

        @pl.when(i == 4)
        def _():
            e_second(1)

        @pl.when(i == 6)
        def _():
            e_third(0)

        @pl.when(i == 7)
        def _():
            e_third(1)

        @pl.when(i == 10)
        def _():
            first()

        now = i == computed[0]
        j = jnp.int32(0)
        for at in computed[1:]:
            now = jnp.logical_or(now, i == at)
            j = j + jnp.where(i >= at, 1, 0)

        @pl.when(now)
        def _():
            compute(j)

        return carry

    lax.fori_loop(0, 2 * (chunks + 3), half_slot, 0)

    lowg[...] = dot_nt(dkv[...], jnp.concatenate([up_pack[j] for j in range(chunks)], axis=1))
    low[...] = (adapter_scale * lowg[...]).astype(BF16)

    def core_copy():
        return remote(A.at[:, 1 - c], A_core, r_send.at[0], r_recv.at[0], CM)

    def reduce_copy(o):
        return remote(A_sum.at[chip(o)], A_recv.at[o], r_send.at[o], r_recv.at[o], chip_device(o))

    def spread_copy(o, index):
        return remote(A_all.at[index, c], A_all.at[index, c], a_send.at[o], a_recv.at[o], chip_device(o))

    def return_copy(c_):
        return remote(A_all.at[:, c_], A_all.at[:, c_], a_send.at[0], a_recv.at[0], CM)

    def adapter_pieces():
        both = (adapter_scale * lowg[...]).T.astype(BF16)

        def down_grad(m, carry):
            for c_ in range(2):
                cols = pl.ds(pl.multiple_of((2 * m + c_) * BLOCK, BLOCK), BLOCK)
                A[m, c_, :, 0:256] = dot(both, E[:, :, cols].reshape(2 * BLOCK, BLOCK)).astype(BF16)
            return carry

        lax.fori_loop(0, 8, down_grad, 0, unroll=2)
        for j in range(chunks):
            up_grad = adapter_scale * dot(low_t[...], dkv[:, j * PACK : j * PACK + PACK])
            for t in range(2):
                A[(j // 2) * 2 + zl, j % 2, 16 * t : 16 * t + 16, 256:384] = up_grad[
                    16 * t : 16 * t + 16, FEATURES * t : FEATURES * t + FEATURES
                ].astype(BF16)

        core_copy().start()

    def adapter_chip():
        core_copy().wait_recv()
        A_sum[...] = (A[:, c].astype(F32) + A_core[...].astype(F32)).astype(BF16)
        for o in range(1, 8):
            reduce_copy(o).start()

    def adapter_sums():
        sum_ = A_sum[me].astype(F32)
        for o in range(1, 8):
            reduce_copy(o).wait_recv()
            sum_ = sum_ + A_recv[o].astype(F32)
        A_all[me, c] = sum_.astype(BF16)
        for o in range(1, 8):
            spread_copy(o, me).start()

    def back_place(i):
        far = jnp.logical_or(i == 2, i == 3)
        dx = jnp.where(far, 2, jnp.where(i < 6, 1 + 2 * lax.rem(i, 2), 0))
        other = jnp.where(far, 3 - i, jnp.where(i < 6, 1 - i // 4, 7 - i))
        return dx, other

    def z_first_copy(a):
        s = z_coords[a][0]
        i = 3 if a == 0 else 2
        return remote(stage.at[i, s], z_first.at[a], zf_send.at[a], zf_recv.at[a], z_peer(a))

    def x_part_copy(d, e, s):
        i = (4 if e == 0 else 0) + d
        return remote(stage.at[i, s], x_part.at[d, e, s], xp_send.at[d, e, s], xp_recv.at[d, e, s], x_peer(1 if d == 0 else 3))

    def z_part_copy(a):
        return remote(z_sum.at[a], z_part.at[a], zp_send.at[a], zp_recv.at[a], z_peer(a))

    def far_copy():
        return remote(z_first_sum, x_far, far_send.at[0], far_recv.at[0], x_peer(2))

    def back(i, carry):
        @pl.when(i == 4)
        def _():
            adapter_pieces()

        @pl.when(i == 6)
        def _():
            adapter_chip()

        dx, other = back_place(i)
        p = lax.rem(x + dx, 4) * 2 + jnp.where(other == 1, 1 - zh, zh)
        for b in range(2):
            r = 2 * p + b
            r_y, r_z, r_c = r // 4, lax.rem(r // 2, 2), lax.rem(r, 2)
            wide = jnp.concatenate([W[j, r_y, r_z, r_c] for j in range(chunks)], axis=1)
            acc = dot_nt(dkv[...], wide)
            acc = acc + dot(low[...], down[:, pl.ds(pl.multiple_of(r * BLOCK, BLOCK), BLOCK)])
            stage[i, :, :, b * BLOCK : (b + 1) * BLOCK] = acc.astype(BF16).reshape(2, BLOCK, BLOCK)

        @pl.when(i == 2)
        def _():
            z_first_copy(2).start()
            z_first_copy(1).start()

        @pl.when(i == 3)
        def _():
            z_first_copy(0).start()

        for d in range(2):
            for e in range(2):

                @pl.when(i == (4 if e == 0 else 0) + d)
                def _(d=d, e=e):
                    x_part_copy(d, e, 1 - zl).start()
                    x_part_copy(d, e, zl).start()

        return carry

    lax.fori_loop(0, 8, back, 0)

    def over_x(e, s):
        sum_ = stage[7 - e, s].astype(F32)
        for d in range(2):
            x_part_copy(d, e, s).wait_recv()
            sum_ = sum_ + x_part[d, e, s].astype(F32)
        return sum_

    def over_x_to(a):
        z_sum[a] = over_x(0 if a == 0 else 1, z_coords[a][0]).astype(BF16)
        z_part_copy(a).start()

    over_x_to(2)
    over_x_to(1)
    total = stage[3, zl].astype(F32)
    for a in range(3):
        z_first_copy(a).wait_recv()
        total = total + z_first[a].astype(F32)
    z_first_sum[...] = total.astype(BF16)
    far_copy().start()

    adapter_sums()
    over_x_to(0)

    def drain(j, carry):
        for n in range(14):
            w_out(j, n).wait_send()
        for t in range(2):
            q_out(j, t).wait_send()
        return carry

    lax.fori_loop(0, chunks, drain, 0)
    for a in range(3):
        ez_out(a).wait_send()
    for d in range(2):
        for k in range(4):
            ex_out(d, k).wait_send()
        for m in range(2):
            ef_out(d, m).wait_send()
    len_copy(zl).wait_send()

    for o in range(1, 8):
        spread_copy(o, chip(8 - o)).wait_recv()
    return_copy(c).start()

    return_copy(1 - c).wait_recv()
    for r in range(16):
        first_up = r // 2 % 2 * half + (r // 4 * 2 + r % 2) * FEATURES
        for t in range(2):
            rows = slice(16 * t, 16 * t + 16)
            down_out[t, :, r * 256 : r * 256 + 256] = A_all[r // 2, r % 2, rows, 0:256].astype(F32)
            up_out[t, :, pl.ds(first_up, FEATURES)] = A_all[r // 2, r % 2, rows, 256:384].astype(F32)
    leave = [
        pltpu.make_async_copy(source.at[t], ref, out_sem.at[n])
        for n, (source, t, ref) in enumerate(
            ((down_out, 0, kd_ref), (up_out, 0, ku_ref), (down_out, 1, vd_ref), (up_out, 1, vu_ref))
        )
    ]
    for copy in leave:
        copy.start()

    total = over_x(0, zl)
    for a in (2, 1, 0):
        z_part_copy(a).wait_recv()
        total = total + z_part[a].astype(F32)
    far_copy().wait_recv()
    out_ref[...] = (total + x_far[...].astype(F32)).astype(BF16)

    for copy in leave:
        copy.wait()
    for a in range(3):
        z_first_copy(a).wait_send()
        z_part_copy(a).wait_send()
    for d in range(2):
        for e in range(2):
            for s in range(2):
                x_part_copy(d, e, s).wait_send()
    far_copy().wait_send()
    core_copy().wait_send()
    for o in range(1, 8):
        reduce_copy(o).wait_send()
        spread_copy(o, me).wait_send()
    return_copy(c).wait_send()


def settle(*refs):
    sources, targets, held, sem = refs[:5], refs[5:10], refs[10:15], refs[15]
    into = [pltpu.make_async_copy(sources[i], held[i], sem.at[0, i]) for i in range(5)]
    out = [pltpu.make_async_copy(held[i], targets[i], sem.at[1, i]) for i in range(5)]
    for copy in into:
        copy.start()
    for i in range(5):
        into[i].wait()
        out[i].start()
    for copy in out:
        copy.wait()


def per_device(
    enc_states, queries, cotangent, enc_lengths, key_weight, value_weight, key_down, key_up, value_down, value_up
):
    inner = queries.shape[2]
    chunks = inner // 2 // FEATURES
    width = key_down.shape[1]
    columns = enc_states.shape[1]
    rows = queries.shape[1]
    hbm = pl.BlockSpec(memory_space=pl.ANY)
    vmem = pl.BlockSpec(memory_space=pltpu.VMEM)
    dma = pltpu.SemaphoreType.DMA
    piece = (BLOCK, columns)
    results = pl.pallas_call(
        functools.partial(kernel, chunks),
        out_shape=(
            jax.ShapeDtypeStruct((BLOCK, columns), BF16),
            jax.ShapeDtypeStruct((16, width), F32),
            jax.ShapeDtypeStruct((16, inner), F32),
            jax.ShapeDtypeStruct((16, width), F32),
            jax.ShapeDtypeStruct((16, inner), F32),
        ),
        in_specs=[hbm, hbm, hbm, pl.BlockSpec(memory_space=pltpu.SMEM)] + [hbm] * 6,
        out_specs=(vmem,) + (hbm,) * 4,
        scratch_shapes=[
            pltpu.VMEM((chunks, 4, 2, 2, BLOCK, PACK), BF16),
            pltpu.VMEM((2, BLOCK, width), BF16),
            pltpu.VMEM((chunks, 2, rows, PACK), BF16),
            pltpu.VMEM((2, 8, 128), jnp.int32),
            pltpu.VMEM((32, width), BF16),
            pltpu.VMEM((2, 16, inner // 2), BF16),
            pltpu.VMEM((chunks, 32, PACK), BF16),
            pltpu.VMEM((2 * BLOCK, 32), BF16),
            pltpu.VMEM((32, 2 * BLOCK), BF16),
            pltpu.VMEM((2 * BLOCK, 32), F32),
            pltpu.VMEM((2 * BLOCK, chunks * PACK), BF16),
            pltpu.VMEM((8, 2) + piece, BF16),
            pltpu.VMEM((2, 2, 2) + piece, BF16),
            pltpu.VMEM((3,) + piece, BF16),
            pltpu.VMEM(piece, BF16),
            pltpu.VMEM((3,) + piece, BF16),
            pltpu.VMEM((3,) + piece, BF16),
            pltpu.VMEM(piece, BF16),
            pltpu.VMEM((8, 2, 32, 384), BF16),
            pltpu.VMEM((8, 32, 384), BF16),
            pltpu.VMEM((8, 32, 384), BF16),
            pltpu.VMEM((8, 32, 384), BF16),
            pltpu.VMEM((8, 2, 32, 384), BF16),
            pltpu.VMEM((2, 16, width), F32),
            pltpu.VMEM((2, 16, inner), F32),
            dma((5,)),
            dma((4,)),
            dma((chunks, 2)),
            dma((chunks, 2)),
            dma((chunks, 14)),
            dma((chunks, 14)),
            dma((chunks, 2)),
            dma((chunks, 2)),
            dma((3,)),
            dma((3,)),
            dma((2, 4)),
            dma((2, 4)),
            dma((2, 2)),
            dma((2, 2)),
            dma((1,)),
            dma((1,)),
            dma((3,)),
            dma((3,)),
            dma((2, 2, 2)),
            dma((2, 2, 2)),
            dma((3,)),
            dma((3,)),
            dma((1,)),
            dma((1,)),
            dma((8,)),
            dma((8,)),
            dma((8,)),
            dma((8,)),
        ],
        compiler_params=pltpu.CompilerParams(
            collective_id=0, has_side_effects=True, vmem_limit_bytes=60 * 1024 * 1024
        ),
        name="adapter_backward",
    )(
        enc_states, queries, cotangent, enc_lengths, key_weight, value_weight,
        key_down[0].T, key_up, value_down[0].T, value_up,
    )
    out, kd_grad, ku_grad, vd_grad, vu_grad = pl.pallas_call(
        settle,
        out_shape=tuple(jax.ShapeDtypeStruct(r.shape, r.dtype) for r in results),
        in_specs=[hbm] * 5,
        out_specs=(hbm,) * 5,
        scratch_shapes=[pltpu.VMEM(r.shape, r.dtype) for r in results] + [dma((2, 5))],
        name="results",
    )(*results)
    return out, kd_grad.T[None], ku_grad[None], vd_grad.T[None], vu_grad[None]


def solution(mesh):
    return jax.shard_map(
        per_device,
        mesh=mesh,
        in_specs=(
            P("dp", "section"),
            P("section", "dp", None),
            P("section", "dp", None),
            P("dp"),
            P("section", "dp", None),
            P("section", "dp", None),
            P("section", None, None),
            P("section", None, None),
            P("section", None, None),
            P("section", None, None),
        ),
        out_specs=(
            P("dp", "section"),
            P("section", None, None),
            P("section", None, None),
            P("section", None, None),
            P("section", None, None),
        ),
        check_vma=False,
    )
```
